512 devices in a mesh: slab: 8 (over y_lo, x), tile: 64 (over z, y_hi, core).
Axes of the slice: x: 4, y: 4 (y_hi: 2, y_lo: 2; y = y_hi * 2 + y_lo), z: 16, core: 2. Of those that a mesh axis runs over, the one named last changes fastest.
Arguments:
- phase: float32 [8, 4096, 2048], P('slab', 'tile'), may hold values from -3.140625 to 3.140625
- absorption: float32 [8, 4096, 2048], P('slab', 'tile'), may hold values from 0.02 to 0.5
- probe: bfloat16 [2, 512, 512], replicated, may hold values from -3 to 3
- taps: bfloat16 [2, 65], replicated, as said below
- offsets: int32 [2, 16], replicated, may hold values from 0 to 1536, as said below
- intensity: float32 [2, 512, 8, 2, 512], P(None, 'tile'), may hold values from 0.05 to 4
Outputs:
- object_grad: float32 [8, 2, 4096, 2048], P('slab', None, 'tile')
The draws below stay inside these ranges and needn't reach their ends.
Inputs may be any that keep to these rules, and one draw needn't show every extreme that they name: offsets[b, g * 2 + q] is the first object column of the window of position q of row band g in batch b. `taps`: tap m acts at offset m - 32.
All inputs are finite; a program needn't handle non-finite values.
Results may differ from the reference program's by a relative error of at most 0.04.
Values may be sent and summed in bfloat16 or wider, within the bound.
A program may use at most 64 MiB of HBM per device.

```python
import math
import jax
import jax.numpy as jnp
from jax import lax

WIN = 512
HALF = 32
NXO = 2048
POS_BAND = 2
BATCHES = 2
SLICES = 8
NYO = 4096
BANDS = 8
BATCH_POS = 16


def draw_taps(key, part):
    width = 2 * HALF + 1
    first_key, second_key = jax.random.split(key)
    spacing = jnp.arange(width, dtype=jnp.float32) - HALF
    jitter = jax.random.uniform(first_key, (width,), jnp.float32, -0.4, 0.4)
    modulus = jax.random.uniform(second_key, (width,), jnp.float32, 0.8, 1.2) / jnp.sqrt(jnp.float32(width))
    angles = 3.14159265 * spacing * spacing / width + jitter
    values = jnp.stack([modulus * jnp.cos(angles), modulus * jnp.sin(angles)])
    return values.astype(jnp.bfloat16)


def draw_offsets(key, part):
    values = jax.random.randint(key, (BATCHES, BATCH_POS), 0, NXO - WIN + 1, dtype=jnp.int32)
    values = values.at[0, 0].set(0)
    return values.at[BATCHES - 1, BATCH_POS - 1].set(NXO - WIN)


def shard_levels(key, shape, cuts, least, top_value):
    level = 1.0
    for position, parts in cuts:
        draws = jax.random.uniform(jax.random.fold_in(jax.random.fold_in(key, 6), position), (parts,), jnp.float32, least / len(cuts), top_value / len(cuts))
        level = level * jnp.repeat(jnp.exp(draws), shape[position] // parts).reshape((-1,) + (1,) * (len(shape) - 1 - position))
    return level


def scatter_about(key, extent, deviation, reach, kind=jnp.bfloat16):
    return jnp.clip(deviation * jax.random.normal(key, extent, jnp.float32), -reach, reach).astype(kind)


def setup_inputs(seed: int = 0) -> dict:
    arg_keys = jax.random.split(jax.random.key(seed), 7)
    return {
        "phase": jnp.clip(jax.random.uniform(arg_keys[0], (SLICES, NYO, NXO), jnp.float32, -3.140625, 3.140625), -3.140625, 3.140625),
        "absorption": jnp.clip(jnp.exp(math.log(0.5) - 3.218876 * jax.random.uniform(arg_keys[1], (SLICES, NYO, NXO), jnp.float32) ** shard_levels(arg_keys[1], (SLICES, NYO, NXO), ((0, 8), (1, 64)), -0.2, 0.2)), 0.02, 0.5),
        "probe": scatter_about(arg_keys[2], (2, WIN, WIN), 0.5, 3.0),
        "taps": draw_taps(jax.random.fold_in(arg_keys[6], 71), 0),
        "offsets": draw_offsets(jax.random.fold_in(arg_keys[6], 71), 0),
        "intensity": jnp.clip(jnp.exp(math.log(4.0) - 4.3820266 * jax.random.uniform(arg_keys[5], (BATCHES, WIN, BANDS, POS_BAND, WIN), jnp.float32) ** shard_levels(arg_keys[5], (BATCHES, WIN, BANDS, POS_BAND, WIN), ((1, 64),), -0.2, 0.2)), 0.05, 4.0),
    }


exact_mode = lax.Precision.HIGHEST


def to_bfloat(values):
    return lax.optimization_barrier(values.astype(jnp.bfloat16)).astype(jnp.float32)


def band_apply(field_re, field_im, taps_re, taps_im, axis_pos):
    widths = [(0, 0)] * field_re.ndim
    widths[axis_pos] = (HALF, HALF)
    padded_re = jnp.pad(field_re, widths)
    padded_im = jnp.pad(field_im, widths)
    length = field_re.shape[axis_pos]

    def accumulate(member, running):
        shifted_re = lax.dynamic_slice_in_dim(padded_re, member, length, axis_pos)
        shifted_im = lax.dynamic_slice_in_dim(padded_im, member, length, axis_pos)
        return (running[0] + taps_re[member] * shifted_re - taps_im[member] * shifted_im,
                running[1] + taps_re[member] * shifted_im + taps_im[member] * shifted_re)

    empty = jnp.zeros_like(field_re)
    return lax.fori_loop(0, 2 * HALF + 1, accumulate, (empty, empty))


def fourier_tables():
    index_line = jnp.arange(WIN, dtype=jnp.int32)
    product_mod = (index_line[:, None] * index_line[None, :]) % WIN
    angles = product_mod.astype(jnp.float32) * (2.0 * math.pi / WIN)
    return to_bfloat(jnp.cos(angles)), to_bfloat(jnp.sin(angles))


def apply_left(matrix, field):
    return jnp.einsum('yr,prk->pyk', matrix, field, precision=exact_mode)


def apply_right(field, matrix):
    return jnp.einsum('prx,kx->prk', field, matrix, precision=exact_mode)


def scatter_windows(plane, pieces, row_starts, col_starts):
    def place(member, running):
        current = lax.dynamic_slice(running, (row_starts[member], col_starts[member]), (WIN, WIN))
        return lax.dynamic_update_slice(running, current + pieces[member], (row_starts[member], col_starts[member]))

    return lax.fori_loop(0, pieces.shape[0], place, plane)


def reference(phase, absorption, probe, taps, offsets, intensity):
    taps_re = taps[0].astype(jnp.float32)
    taps_im = taps[1].astype(jnp.float32)
    back_re = taps_re[::-1]
    back_im = -taps_im[::-1]
    cos_table, sin_table = fourier_tables()
    norm_scale = WIN ** -0.5
    decay = jnp.exp(-absorption)
    plain_re = decay * jnp.cos(phase)
    plain_im = decay * jnp.sin(phase)
    row_shift = WIN // 2
    trans_re = jnp.roll(plain_re, -row_shift, axis=1)
    trans_im = jnp.roll(plain_im, -row_shift, axis=1)
    row_starts = (jnp.arange(BATCH_POS, dtype=jnp.int32) // POS_BAND) * WIN
    grad_re = jnp.zeros_like(trans_re)
    grad_im = jnp.zeros_like(trans_re)
    for batch in range(BATCHES):
        col_starts = offsets[batch].astype(jnp.int32)

        def windows(field):
            return jax.vmap(lambda row_at, col_at: lax.dynamic_slice(field, (row_at, col_at), (WIN, WIN)))(row_starts, col_starts)

        wave_re = jnp.broadcast_to(probe[0].astype(jnp.float32), (BATCH_POS, WIN, WIN))
        wave_im = jnp.broadcast_to(probe[1].astype(jnp.float32), (BATCH_POS, WIN, WIN))
        kept = []
        for layer in range(SLICES):
            kept.append((wave_re, wave_im))
            win_re = windows(trans_re[layer])
            win_im = windows(trans_im[layer])
            lit_re = to_bfloat(wave_re * win_re - wave_im * win_im)
            lit_im = to_bfloat(wave_re * win_im + wave_im * win_re)
            mid_re, mid_im = band_apply(lit_re, lit_im, taps_re, taps_im, 1)
            mid_re, mid_im = to_bfloat(mid_re), to_bfloat(mid_im)
            wave_re, wave_im = band_apply(mid_re, mid_im, taps_re, taps_im, 2)
            wave_re, wave_im = to_bfloat(wave_re), to_bfloat(wave_im)
        spec_re = to_bfloat((apply_right(wave_re, cos_table) + apply_right(wave_im, sin_table)) * norm_scale)
        spec_im = to_bfloat((apply_right(wave_im, cos_table) - apply_right(wave_re, sin_table)) * norm_scale)
        far_re = (apply_left(cos_table, spec_re) + apply_left(sin_table, spec_im)) * norm_scale
        far_im = (apply_left(cos_table, spec_im) - apply_left(sin_table, spec_re)) * norm_scale
        measured = jnp.transpose(intensity[batch].reshape(WIN, BATCH_POS, WIN), (1, 2, 0))
        excess = far_re * far_re + far_im * far_im - measured
        err_re = to_bfloat(excess * far_re)
        err_im = to_bfloat(excess * far_im)
        spec_back_re = to_bfloat((apply_left(cos_table.T, err_re) - apply_left(sin_table.T, err_im)) * norm_scale)
        spec_back_im = to_bfloat((apply_left(cos_table.T, err_im) + apply_left(sin_table.T, err_re)) * norm_scale)
        gwave_re = to_bfloat((apply_right(spec_back_re, cos_table.T) - apply_right(spec_back_im, sin_table.T)) * norm_scale)
        gwave_im = to_bfloat((apply_right(spec_back_im, cos_table.T) + apply_right(spec_back_re, sin_table.T)) * norm_scale)
        for layer in reversed(range(SLICES)):
            gmid_re, gmid_im = band_apply(gwave_re, gwave_im, back_re, back_im, 2)
            gmid_re, gmid_im = to_bfloat(gmid_re), to_bfloat(gmid_im)
            glit_re, glit_im = band_apply(gmid_re, gmid_im, back_re, back_im, 1)
            seen_re, seen_im = kept[layer]
            inc_re = glit_re * seen_re + glit_im * seen_im
            inc_im = glit_im * seen_re - glit_re * seen_im
            grad_re = grad_re.at[layer].set(scatter_windows(grad_re[layer], inc_re, row_starts, col_starts))
            grad_im = grad_im.at[layer].set(scatter_windows(grad_im[layer], inc_im, row_starts, col_starts))
            win_re = windows(trans_re[layer])
            win_im = windows(trans_im[layer])
            gwave_re = to_bfloat(win_re * glit_re + win_im * glit_im)
            gwave_im = to_bfloat(win_re * glit_im - win_im * glit_re)
    grad_re = jnp.roll(grad_re, row_shift, axis=1)
    grad_im = jnp.roll(grad_im, row_shift, axis=1)
    phase_grad = grad_im * plain_re - grad_re * plain_im
    absorb_grad = -(grad_re * plain_re + grad_im * plain_im)
    return jnp.stack([phase_grad, absorb_grad], axis=1)
```

```python
import functools
import math

import jax
import jax.numpy as jnp
import numpy as np
from jax import lax
from jax.experimental import pallas as pl
from jax.experimental.pallas import tpu as pltpu
from jax.sharding import PartitionSpec as P

MESH = pl.DeviceIdType.MESH
F32 = jnp.float32
BF16 = jnp.bfloat16
WIN = 512
HALF = 32
NXO = 2048
SLICES = 8
STRIP = 64
ROWS = 128
SCALE = WIN**-0.5


def dot(a, b):
    return jnp.dot(a, b, preferred_element_type=F32)


def fourier_tables():
    line = np.arange(WIN)
    angles = (line[:, None] * line[None, :] % WIN).astype(np.float64) * (2.0 * math.pi / WIN)
    return np.cos(angles).astype(np.float32), np.sin(angles).astype(np.float32)


def sincos(x):
    h = 0.5 * x
    q = h * h
    s = -2.50521084e-8
    for term in (2.75573192e-6, -1.98412698e-4, 8.33333333e-3, -1.66666667e-1, 1.0):
        s = s * q + term
    s = s * h
    c = 2.08767570e-9
    for term in (-2.75573192e-7, 2.48015873e-5, -1.38888889e-3, 4.16666667e-2, -0.5, 1.0):
        c = c * q + term
    return 2.0 * s * c, 1.0 - 2.0 * s * s


def prepare_kernel(info, phase, absorb, intensity, win, trans, ints, wide):
    for part in range(4):
        rows = pl.ds(part * 16, 16)
        sin_part, cos_part = sincos(phase[rows, :])
        decay = jnp.exp(-absorb[rows, :])
        real, imag = decay * cos_part, decay * sin_part
        trans[0, rows, :] = real
        trans[1, rows, :] = imag
        wide[0, rows, :NXO] = real
        wide[1, rows, :NXO] = imag
    wide[:, :, NXO:] = jnp.zeros((2, STRIP, 128), F32)
    for p in range(4):
        start = info[p]
        base = pl.multiple_of(start // 128 * 128, 128)
        turn = (640 - start % 128) % 640
        for part in range(2):
            block = wide[part, :, pl.ds(base, 640)]
            win[p, part] = pltpu.roll(block, turn, 1)[:, :WIN].astype(BF16)
        ints[p] = intensity[p // 2, :, 0, p % 2, :]


def prepare(info, phase, absorb, intensity):
    vmem = pl.BlockSpec(memory_space=pltpu.VMEM)
    return pl.pallas_call(
        prepare_kernel,
        grid_spec=pltpu.PrefetchScalarGridSpec(
            num_scalar_prefetch=1,
            grid=(1,),
            in_specs=[
                pl.BlockSpec((STRIP, NXO), lambda i, info: (0, 0)),
                pl.BlockSpec((STRIP, NXO), lambda i, info: (0, 0)),
                pl.BlockSpec((2, 8, 1, 2, WIN), lambda i, info: (0, 0, info[4], 0, 0)),
            ],
            out_specs=[
                pl.BlockSpec((4, 2, STRIP, WIN), lambda i, info: (0, 0, 0, 0)),
                pl.BlockSpec((2, STRIP, NXO), lambda i, info: (0, 0, 0)),
                pl.BlockSpec((4, 8, WIN), lambda i, info: (0, 0, 0)),
            ],
            scratch_shapes=[pltpu.VMEM((2, STRIP, NXO + 128), F32)],
        ),
        out_shape=[
            jax.ShapeDtypeStruct((4, 2, STRIP, WIN), BF16),
            jax.ShapeDtypeStruct((2, STRIP, NXO), F32),
            jax.ShapeDtypeStruct((4, 8, WIN), F32),
        ],
        compiler_params=pltpu.CompilerParams(vmem_limit_bytes=32 << 20),
        name="prepare",
    )(info, phase, absorb, intensity)


def finish_kernel(info, inc, trans, out, wide):
    wide[...] = jnp.zeros_like(wide)
    blank = jnp.zeros((STRIP, 128), F32)
    for p in range(4):
        start = info[p]
        base = pl.multiple_of(start // 128 * 128, 128)
        for part in range(2):
            block = jnp.concatenate([inc[p, part].astype(F32), blank], axis=1)
            wide[part, :, pl.ds(base, 640)] += pltpu.roll(block, start % 128, 1)
    real, imag = trans[0], trans[1]
    grad_re, grad_im = wide[0, :, :NXO], wide[1, :, :NXO]
    out[0] = grad_im * real - grad_re * imag
    out[1] = -(grad_re * real + grad_im * imag)


def finish(info, inc, trans):
    vmem = pl.BlockSpec(memory_space=pltpu.VMEM)
    return pl.pallas_call(
        finish_kernel,
        in_specs=[pl.BlockSpec(memory_space=pltpu.SMEM), vmem, vmem],
        out_specs=vmem,
        out_shape=jax.ShapeDtypeStruct((2, STRIP, NXO), F32),
        scratch_shapes=[pltpu.VMEM((2, STRIP, NXO + 128), F32)],
        compiler_params=pltpu.CompilerParams(vmem_limit_bytes=32 << 20),
        name="finish",
    )(info, inc, trans)


def device_at(x, y, z, core):
    return ((y % 2) * 4 + x, (z % 16) * 4 + (y // 2) * 2 + core)


def member_at(band, p, c):
    upper = c // 2
    return device_at(p, 0 * p, 2 * band + 1 + upper, (c + upper) % 2)


def strip_at(band, layer, w):
    return (layer, (band * 8 + 4 + w) % 64)


def same(a, b):
    return (a[0] == b[0]) & (a[1] == b[1])


def chain_kernel(
    win, ints, probe, line, cos_hbm, sin_hbm, out,
    trans, waves, lits, gmids, incs, halo, acc, gwave,
    row_own, row_halo, col_w, cos_t, sin_t, int_in, int_t,
    stage, spec_in, back_out, back_in,
    win_send, win_recv, int_send, int_recv, halo_send, halo_recv,
    inc_send, inc_recv, spec_send, spec_recv, back_send, back_recv, table_sem,
):
    slab = lax.axis_index("slab")
    tile = lax.axis_index("tile")
    me = (slab, tile)
    band = ((tile + 60) % 64) // 8
    w = (tile + 60) % 8
    x, y = slab % 4, (tile // 2) % 2 * 2 + slab // 4
    upper = w // 4
    is_member = y == 0
    p_me = x
    c_me = upper * 2 + (tile % 2 + upper) % 2

    def signal(device):
        pl.semaphore_signal(pltpu.get_barrier_semaphore(), 1, device_id=device, device_id_type=MESH)

    @pl.when(is_member)
    def _():
        def greet(i, _):
            signal(strip_at(band, i // 2, 2 * c_me + i % 2))
            signal((band, 16 * c_me + i))
            return 0

        lax.fori_loop(0, 16, greet, 0)
        for d in range(1, 4):
            signal(member_at(band, p_me, (c_me + d) % 4))

    for p in range(4):
        signal(member_at(band, jnp.int32(p), w // 2))
    barrier = pltpu.get_barrier_semaphore()

    @pl.when(is_member)
    def _():
        pl.semaphore_wait(barrier, 16 + 3 + 8)

    @pl.when(jnp.logical_not(is_member))
    def _():
        pl.semaphore_wait(barrier, 8)

    half = pl.ds(pl.multiple_of((w % 2) * STRIP, STRIP), STRIP)
    for p in range(4):
        target = member_at(band, jnp.int32(p), w // 2)

        @pl.when(same(target, me))
        def _():
            pltpu.make_async_copy(
                win.at[p], trans.at[slab, :, half, :], win_recv.at[slab, w % 2]
            ).start()

        @pl.when(jnp.logical_not(same(target, me)))
        def _():
            pltpu.make_async_remote_copy(
                src_ref=win.at[p],
                dst_ref=trans.at[slab, :, half, :],
                send_sem=win_send.at[p],
                recv_sem=win_recv.at[slab, w % 2],
                device_id=target,
                device_id_type=MESH,
            ).start()

    for p in range(4):
        target = member_at(slab, jnp.int32(p), tile // 16)

        @pl.when(same(target, me))
        def _():
            pltpu.make_async_copy(
                ints.at[p], int_in.at[tile % 16], int_recv.at[tile % 16]
            ).start()

        @pl.when(jnp.logical_not(same(target, me)))
        def _():
            pltpu.make_async_remote_copy(
                src_ref=ints.at[p],
                dst_ref=int_in.at[tile % 16],
                send_sem=int_send.at[p],
                recv_sem=int_recv.at[tile % 16],
                device_id=target,
                device_id_type=MESH,
            ).start()

    def toeplitz(row, shift):
        lanes = jnp.broadcast_to(line[row : row + 1, :], (128, 256))
        return pltpu.roll(lanes, shift, 1, stride=1, stride_axis=0)

    def build(direction):
        plain, turned = (0, 2) if direction == 0 else (2, 0)
        sign = 1.0 if direction == 0 else -1.0
        real = toeplitz(plain, 224)
        imag = sign * toeplitz(plain + 1, 224)
        row_own[direction, :128, :128] = real[:, :128].astype(BF16)
        row_own[direction, :128, 128:] = (-imag[:, :128]).astype(BF16)
        row_own[direction, 128:, :128] = imag[:, :128].astype(BF16)
        row_own[direction, 128:, 128:] = real[:, :128].astype(BF16)
        rim_re, rim_im = real[:, 128:], imag[:, 128:]
        lane = lax.broadcasted_iota(jnp.int32, (128, 128), 1)

        def weave(first, second):
            low = jnp.where(lane < 32, first, pltpu.roll(first, 64, 1))
            high = jnp.where(lane < 96, pltpu.roll(second, 64, 1), second)
            return jnp.where(lane < 64, low, high)

        row_halo[direction, :128, :] = weave(rim_re, -rim_im).astype(BF16)
        row_halo[direction, 128:, :] = weave(rim_im, rim_re).astype(BF16)
        for part in range(2):
            factor = 1.0 if part == 0 else sign
            far_part = factor * toeplitz(turned + part, 96)[:, :128]
            near_part = factor * toeplitz(turned + part, 224)[:, :128]
            columns = pl.ds(part * 128, 128)
            col_w[direction, :128, columns] = jnp.where(lane < 32, far_part, 0.0).astype(BF16)
            col_w[direction, 128:256, columns] = near_part.astype(BF16)
            col_w[direction, 256:, columns] = jnp.where(lane >= 96, far_part, 0.0).astype(BF16)

    def along_columns(field, direction):
        reals, imags = [], []
        for j in range(4):
            low, high = max(0, j - 1), min(4, j + 2)
            weights = col_w[direction, (low - j + 1) * 128 : (high - j + 1) * 128, :]
            both = dot(field[:, low * 128 : high * 128], weights)
            reals.append(both[:128, :128] - both[128:, 128:])
            imags.append(both[:128, 128:] + both[128:, :128])
        return jnp.concatenate(reals, axis=1), jnp.concatenate(imags, axis=1)

    def halo_copies(step, field):
        above = pltpu.make_async_remote_copy(
            src_ref=field.at[:, 0:HALF, :],
            dst_ref=halo.at[step, :, 0],
            send_sem=halo_send.at[step, 0],
            recv_sem=halo_recv.at[step, 0],
            device_id=member_at(band, p_me, (c_me + 3) % 4),
            device_id_type=MESH,
        )
        below = pltpu.make_async_remote_copy(
            src_ref=field.at[:, ROWS - HALF : ROWS, :],
            dst_ref=halo.at[step, :, 1],
            send_sem=halo_send.at[step, 1],
            recv_sem=halo_recv.at[step, 1],
            device_id=member_at(band, p_me, (c_me + 1) % 4),
            device_id_type=MESH,
        )
        return above, below

    def halo_start(step, field):
        above, below = halo_copies(step, field)

        @pl.when(c_me > 0)
        def _():
            above.start()

        @pl.when(c_me < 3)
        def _():
            below.start()

    def halo_wait(step, field, sends):
        above, below = halo_copies(step, field)

        @pl.when(c_me < 3)
        def _():
            if sends:
                below.wait_send()
            else:
                above.wait_recv()

        @pl.when(c_me > 0)
        def _():
            if sends:
                above.wait_send()
            else:
                below.wait_recv()

    def along_rows(step, field, direction):
        acc[...] = dot(row_own[direction], field[...].reshape(2 * ROWS, WIN))
        halo_wait(step, field, False)
        rim = halo[step].reshape(4 * HALF, WIN)
        return acc[...] + dot(row_halo[direction], rim)

    @pl.when(is_member)
    def _():
        tables = [
            pltpu.make_async_copy(cos_hbm, cos_t, table_sem.at[0]),
            pltpu.make_async_copy(sin_hbm, sin_t, table_sem.at[1]),
            pltpu.make_async_copy(
                probe.at[:, pl.ds(pl.multiple_of(c_me * ROWS, ROWS), ROWS), :],
                waves.at[0],
                table_sem.at[2],
            ),
        ]
        for copy in tables:
            copy.start()
        build(0)
        build(1)

        @pl.when(c_me == 0)
        def _():
            halo[:, :, 1] = jnp.zeros((16, 2, HALF, WIN), BF16)

        @pl.when(c_me == 3)
        def _():
            halo[:, :, 0] = jnp.zeros((16, 2, HALF, WIN), BF16)

        for copy in tables:
            copy.wait()

        def forward(s, _):
            for j in range(2):
                part = trans.at[s, :, pl.ds(j * STRIP, STRIP), :]
                pltpu.make_async_copy(part, part, win_recv.at[s, j]).wait()
            field = lits.at[s]

            def light(rows):
                wave_re = waves[s, 0, rows, :].astype(F32)
                wave_im = waves[s, 1, rows, :].astype(F32)
                trans_re = trans[s, 0, rows, :].astype(F32)
                trans_im = trans[s, 1, rows, :].astype(F32)
                field[0, rows, :] = (wave_re * trans_re - wave_im * trans_im).astype(BF16)
                field[1, rows, :] = (wave_re * trans_im + wave_im * trans_re).astype(BF16)

            light(pl.ds(0, HALF))
            light(pl.ds(ROWS - HALF, HALF))
            halo_start(s, field)
            light(pl.ds(HALF, ROWS - 2 * HALF))
            mid = along_rows(s, field, 0).astype(BF16)
            real, imag = along_columns(mid, 0)
            waves[s + 1, 0] = real.astype(BF16)
            waves[s + 1, 1] = imag.astype(BF16)
            return 0

        lax.fori_loop(0, SLICES, forward, 0)

        for i in range(16):
            pltpu.make_async_copy(int_in.at[i], int_in.at[i], int_recv.at[i]).wait()
        int_t[...] = int_in[...].reshape(128, WIN).T

        exit_wave = waves[SLICES].reshape(2 * ROWS, WIN)
        by_cos, by_sin = dot(exit_wave, cos_t[...]), dot(exit_wave, sin_t[...])
        spec_re = ((by_cos[:128] + by_sin[128:]) * SCALE).astype(BF16)
        spec_im = ((by_cos[128:] - by_sin[:128]) * SCALE).astype(BF16)
        for k in range(4):
            stage[k, :, :128] = spec_re[:, k * 128 : (k + 1) * 128]
            stage[k, :, 128:] = spec_im[:, k * 128 : (k + 1) * 128]

        mine = pl.ds(pl.multiple_of(c_me * ROWS, ROWS), ROWS)

        def spec_copy(d):
            other = (c_me + d) % 4
            return pltpu.make_async_remote_copy(
                src_ref=stage.at[other],
                dst_ref=spec_in.at[mine, :],
                send_sem=spec_send.at[d],
                recv_sem=spec_recv.at[d],
                device_id=member_at(band, p_me, other),
                device_id_type=MESH,
            )

        for d in range(1, 4):
            spec_copy(d).start()
        spec_in[mine, :] = stage[c_me]
        for d in range(1, 4):
            spec_copy(d).wait()

        spectrum = spec_in[...]
        by_cos, by_sin = dot(cos_t[...], spectrum), dot(sin_t[...], spectrum)
        far_re = (by_cos[:, :128] + by_sin[:, 128:]) * SCALE
        far_im = (by_cos[:, 128:] - by_sin[:, :128]) * SCALE
        excess = far_re * far_re + far_im * far_im - int_t[...]
        err = jnp.concatenate(
            [(excess * far_re).astype(BF16), (excess * far_im).astype(BF16)], axis=1
        )
        by_cos, by_sin = dot(cos_t[...], err), dot(sin_t[...], err)
        back_re = ((by_cos[:, :128] - by_sin[:, 128:]) * SCALE).astype(BF16)
        back_im = ((by_cos[:, 128:] + by_sin[:, :128]) * SCALE).astype(BF16)
        for k in range(4):
            back_out[k, :, :128] = back_re[k * 128 : (k + 1) * 128]
            back_out[k, :, 128:] = back_im[k * 128 : (k + 1) * 128]

        def back_copy(d):
            other = (c_me + d) % 4
            return pltpu.make_async_remote_copy(
                src_ref=back_out.at[other],
                dst_ref=back_in.at[c_me],
                send_sem=back_send.at[d],
                recv_sem=back_recv.at[d],
                device_id=member_at(band, p_me, other),
                device_id_type=MESH,
            )

        for d in range(1, 4):
            back_copy(d).start()
        back_in[c_me] = back_out[c_me]
        for d in range(1, 4):
            back_copy(d).wait()

        back_all = jnp.concatenate(
            [
                jnp.concatenate([back_in[k, :, :128] for k in range(4)], axis=1),
                jnp.concatenate([back_in[k, :, 128:] for k in range(4)], axis=1),
            ],
            axis=0,
        )
        by_cos, by_sin = dot(back_all, cos_t[...]), dot(back_all, sin_t[...])
        gwave[0] = ((by_cos[:128] - by_sin[128:]) * SCALE).astype(BF16)
        gwave[1] = ((by_cos[128:] + by_sin[:128]) * SCALE).astype(BF16)

        def inc_target(s, j):
            return strip_at(band, s, 2 * c_me + j)

        def inc_copy(s, j):
            return pltpu.make_async_remote_copy(
                src_ref=incs.at[s, :, pl.ds(j * STRIP, STRIP), :],
                dst_ref=out.at[p_me],
                send_sem=inc_send.at[s, j],
                recv_sem=inc_recv.at[p_me],
                device_id=inc_target(s, j),
                device_id_type=MESH,
            )

        def backward(i, _):
            s = SLICES - 1 - i
            step = SLICES + s
            field = gmids.at[s]
            real, imag = along_columns(gwave[...].reshape(2 * ROWS, WIN), 1)
            field[0] = real.astype(BF16)
            field[1] = imag.astype(BF16)
            halo_start(step, field)
            glit = along_rows(step, field, 1)
            glit_re, glit_im = glit[:128], glit[128:]
            seen_re = waves[s, 0].astype(F32)
            seen_im = waves[s, 1].astype(F32)
            incs[s, 0] = (glit_re * seen_re + glit_im * seen_im).astype(BF16)
            incs[s, 1] = (glit_im * seen_re - glit_re * seen_im).astype(BF16)
            for j in range(2):
                local = same(inc_target(s, j), me)

                @pl.when(local)
                def _():
                    pltpu.make_async_copy(
                        incs.at[s, :, pl.ds(j * STRIP, STRIP), :], out.at[p_me], inc_recv.at[p_me]
                    ).start()

                @pl.when(jnp.logical_not(local))
                def _():
                    inc_copy(s, j).start()

            trans_re = trans[s, 0].astype(F32)
            trans_im = trans[s, 1].astype(F32)
            gwave[0] = (trans_re * glit_re + trans_im * glit_im).astype(BF16)
            gwave[1] = (trans_re * glit_im - trans_im * glit_re).astype(BF16)
            return 0

        lax.fori_loop(0, SLICES, backward, 0)

        def settle(s, _):
            halo_wait(s, lits.at[s], True)
            halo_wait(SLICES + s, gmids.at[s], True)
            for j in range(2):

                @pl.when(jnp.logical_not(same(inc_target(s, j), me)))
                def _():
                    inc_copy(s, j).wait_send()

            return 0

        lax.fori_loop(0, SLICES, settle, 0)

    for p in range(4):

        @pl.when(jnp.logical_not(same(member_at(band, jnp.int32(p), w // 2), me)))
        def _():
            pltpu.make_async_copy(win.at[p], win.at[p], win_send.at[p]).wait()

        @pl.when(jnp.logical_not(same(member_at(slab, jnp.int32(p), tile // 16), me)))
        def _():
            pltpu.make_async_copy(ints.at[p], ints.at[p], int_send.at[p]).wait()

        pltpu.make_async_copy(out.at[p], out.at[p], inc_recv.at[p]).wait()


def chain(win, ints, probe, line):
    hbm = pl.BlockSpec(memory_space=pl.ANY)
    vmem = pl.BlockSpec(memory_space=pltpu.VMEM)
    cos_table, sin_table = (jnp.asarray(t, BF16) for t in fourier_tables())
    dma = pltpu.SemaphoreType.DMA
    group = (2, ROWS, WIN)
    return pl.pallas_call(
        chain_kernel,
        in_specs=[hbm, hbm, hbm, vmem, hbm, hbm],
        out_specs=hbm,
        out_shape=jax.ShapeDtypeStruct((4, 2, STRIP, WIN), BF16),
        scratch_shapes=[
            pltpu.VMEM((SLICES,) + group, BF16),
            pltpu.VMEM((SLICES + 1,) + group, BF16),
            pltpu.VMEM((SLICES,) + group, BF16),
            pltpu.VMEM((SLICES,) + group, BF16),
            pltpu.VMEM((SLICES,) + group, BF16),
            pltpu.VMEM((2 * SLICES, 2, 2, HALF, WIN), BF16),
            pltpu.VMEM((2 * ROWS, WIN), F32),
            pltpu.VMEM(group, BF16),
            pltpu.VMEM((2, 256, 256), BF16),
            pltpu.VMEM((2, 256, 128), BF16),
            pltpu.VMEM((2, 384, 256), BF16),
            pltpu.VMEM((WIN, WIN), BF16),
            pltpu.VMEM((WIN, WIN), BF16),
            pltpu.VMEM((16, 8, WIN), F32),
            pltpu.VMEM((WIN, 128), F32),
            pltpu.VMEM((4, 128, 256), BF16),
            pltpu.VMEM((WIN, 256), BF16),
            pltpu.VMEM((4, 128, 256), BF16),
            pltpu.VMEM((4, 128, 256), BF16),
            dma((4,)),
            dma((SLICES, 2)),
            dma((4,)),
            dma((16,)),
            dma((2 * SLICES, 2)),
            dma((2 * SLICES, 2)),
            dma((SLICES, 2)),
            dma((4,)),
            dma((4,)),
            dma((4,)),
            dma((4,)),
            dma((4,)),
            dma((3,)),
        ],
        compiler_params=pltpu.CompilerParams(
            collective_id=0, has_side_effects=True, vmem_limit_bytes=48 << 20
        ),
        name="chain",
    )(win, ints, probe, line, cos_table, sin_table)


def on_device(phase, absorption, probe, taps, offsets, intensity):
    slab = lax.axis_index("slab")
    band = ((lax.axis_index("tile") + 60) % 64) // 8
    starts = lax.dynamic_slice_in_dim(offsets, band * 2, 2, 1).reshape(4)
    info = jnp.concatenate([starts, slab[None].astype(jnp.int32)])
    both = jnp.concatenate([taps, taps[:, ::-1]], axis=0).astype(F32)
    line = jnp.pad(both, ((0, 4), (0, 256 - both.shape[1])))
    win, trans, ints = prepare(info, phase[0], absorption[0], intensity)
    inc = chain(win, ints, probe, line)
    return finish(info, inc, trans)[None]


def solution(mesh):
    placed = (
        P("slab", "tile", None),
        P("slab", "tile", None),
        P(),
        P(),
        P(),
        P(None, "tile", None, None, None),
    )
    return jax.shard_map(
        on_device,
        mesh=mesh,
        in_specs=placed,
        out_specs=P("slab", None, "tile", None),
        check_vma=False,
    )
```

```python
import functools
import math

import jax
import jax.numpy as jnp
import numpy as np
from jax import lax
from jax.experimental import pallas as pl
from jax.experimental.pallas import tpu as pltpu
from jax.sharding import PartitionSpec as P

MESH = pl.DeviceIdType.MESH
F32 = jnp.float32
BF16 = jnp.bfloat16
WIN = 512
HALF = 32
NXO = 2048
SLICES = 8
STRIP = 64
AHEAD = 4
ROWS = 128
SCALE = WIN**-0.5


def dot(a, b):
    return jnp.dot(a, b, preferred_element_type=F32)


def fourier_tables():
    line = np.arange(WIN)
    angles = (line[:, None] * line[None, :] % WIN).astype(np.float64) * (2.0 * math.pi / WIN)
    return np.cos(angles).astype(np.float32), np.sin(angles).astype(np.float32)


def sincos(x):
    h = 0.5 * x
    q = h * h
    s = -2.50521084e-8
    for term in (2.75573192e-6, -1.98412698e-4, 8.33333333e-3, -1.66666667e-1, 1.0):
        s = s * q + term
    s = s * h
    c = 2.08767570e-9
    for term in (-2.75573192e-7, 2.48015873e-5, -1.38888889e-3, 4.16666667e-2, -0.5, 1.0):
        c = c * q + term
    return 2.0 * s * c, 1.0 - 2.0 * s * s


CHUNK = 16


def prepare_kernel(info, phase, absorb, intensity, win, trans, ints, wide):
    sin_part, cos_part = sincos(phase[...])
    decay = jnp.exp(-absorb[...])
    real, imag = decay * cos_part, decay * sin_part
    trans[0] = real
    trans[1] = imag
    wide[0, :, :NXO] = real
    wide[1, :, :NXO] = imag
    wide[:, :, NXO:] = jnp.zeros((2, CHUNK, 128), F32)
    for p in range(4):
        start = info[p]
        base = pl.multiple_of(start // 128 * 128, 128)
        turn = (640 - start % 128) % 640
        for part in range(2):
            block = wide[part, :, pl.ds(base, 640)]
            win[p, part] = pltpu.roll(block, turn, 1)[:, :WIN].astype(BF16)

    @pl.when(pl.program_id(0) == 0)
    def _():
        for p in range(4):
            values = intensity[p // 2, :, 0, p % 2, :]
            halves = [values[:, : WIN // 2], values[:, WIN // 2 :]]
            ints[p] = jnp.concatenate(halves, axis=0).astype(BF16)


def prepare(info, phase, absorb, intensity):
    return pl.pallas_call(
        prepare_kernel,
        grid_spec=pltpu.PrefetchScalarGridSpec(
            num_scalar_prefetch=1,
            grid=(STRIP // CHUNK,),
            in_specs=[
                pl.BlockSpec((CHUNK, NXO), lambda i, info: (i, 0)),
                pl.BlockSpec((CHUNK, NXO), lambda i, info: (i, 0)),
                pl.BlockSpec((2, 8, 1, 2, WIN), lambda i, info: (0, 0, info[4], 0, 0)),
            ],
            out_specs=[
                pl.BlockSpec((4, 2, CHUNK, WIN), lambda i, info: (0, 0, i, 0)),
                pl.BlockSpec((2, CHUNK, NXO), lambda i, info: (0, i, 0)),
                pl.BlockSpec((4, 16, WIN // 2), lambda i, info: (0, 0, 0)),
            ],
            scratch_shapes=[pltpu.VMEM((2, CHUNK, NXO + 128), F32)],
        ),
        out_shape=[
            jax.ShapeDtypeStruct((4, 2, STRIP, WIN), BF16),
            jax.ShapeDtypeStruct((2, STRIP, NXO), F32),
            jax.ShapeDtypeStruct((4, 16, WIN // 2), BF16),
        ],
        compiler_params=pltpu.CompilerParams(vmem_limit_bytes=60 << 20),
        name="prepare",
    )(info, phase, absorb, intensity)


def finish_kernel(info, inc, trans, out, wide):
    wide[...] = jnp.zeros_like(wide)
    blank = jnp.zeros((STRIP, 128), F32)
    for p in range(4):
        start = info[p]
        base = pl.multiple_of(start // 128 * 128, 128)
        for part in range(2):
            block = jnp.concatenate([inc[p, part].astype(F32), blank], axis=1)
            wide[part, :, pl.ds(base, 640)] += pltpu.roll(block, start % 128, 1)
    real, imag = trans[0], trans[1]
    grad_re, grad_im = wide[0, :, :NXO], wide[1, :, :NXO]
    out[0] = grad_im * real - grad_re * imag
    out[1] = -(grad_re * real + grad_im * imag)


def finish(info, inc, trans):
    vmem = pl.BlockSpec(memory_space=pltpu.VMEM)
    return pl.pallas_call(
        finish_kernel,
        in_specs=[pl.BlockSpec(memory_space=pltpu.SMEM), vmem, vmem],
        out_specs=vmem,
        out_shape=jax.ShapeDtypeStruct((2, STRIP, NXO), F32),
        scratch_shapes=[pltpu.VMEM((2, STRIP, NXO + 128), F32)],
        compiler_params=pltpu.CompilerParams(vmem_limit_bytes=32 << 20),
        name="finish",
    )(info, inc, trans)


def device_at(x, y, z, core):
    return ((y % 2) * 4 + x, (z % 16) * 4 + (y // 2) * 2 + core)


def member_at(band, p, c):
    upper = c // 2
    return device_at(p, p, 2 * band + 1 + upper, (c + upper) % 2)


def strip_at(band, layer, w):
    return (layer, (band * 8 + 4 + w) % 64)


def same(a, b):
    return (a[0] == b[0]) & (a[1] == b[1])


def chain_kernel(
    win, ints, probe, taps, cos_hbm, sin_hbm, out,
    line, trans, waves, lits, gmids, incs, halo, acc, gwave,
    row_rim, row_core, row_halo, col_w, cos_t, sin_t, int_in, int_t,
    stage, spec_in, back_out, back_in,
    credit, win_send, win_recv, int_send, int_recv, halo_send, halo_recv,
    inc_send, inc_recv, spec_send, spec_recv, back_send, back_recv, table_sem,
):
    slab = lax.axis_index("slab")
    tile = lax.axis_index("tile")
    me = (slab, tile)
    band = ((tile + 60) % 64) // 8
    w = (tile + 60) % 8
    x, y = slab % 4, (tile // 2) % 2 * 2 + slab // 4
    upper = w // 4
    is_member = y == x
    p_me = x
    c_me = upper * 2 + (tile % 2 + upper) % 2

    def signal(device):
        pl.semaphore_signal(pltpu.get_barrier_semaphore(), 1, device_id=device, device_id_type=MESH)

    @pl.when(is_member)
    def _():
        def greet(i, _):
            signal(strip_at(band, i // 2, 2 * c_me + i % 2))
            signal((band, 16 * c_me + i))
            return 0

        lax.fori_loop(0, 16, greet, 0)
        for d in range(1, 4):
            signal(member_at(band, p_me, (c_me + d) % 4))

    for p in range(4):
        signal(member_at(band, jnp.int32(p), w // 2))
    barrier = pltpu.get_barrier_semaphore()

    @pl.when(is_member)
    def _():
        pl.semaphore_wait(barrier, 16 + 3 + 8)

    @pl.when(jnp.logical_not(is_member))
    def _():
        pl.semaphore_wait(barrier, 8)

    half = pl.ds(pl.multiple_of((w % 2) * STRIP, STRIP), STRIP)

    def hand_out():
        for p in range(4):
            target = member_at(band, jnp.int32(p), w // 2)

            @pl.when(same(target, me))
            def _():
                pltpu.make_async_copy(
                    win.at[p], trans.at[slab, :, half, :], win_recv.at[slab, w % 2]
                ).start()

            @pl.when(jnp.logical_not(same(target, me)))
            def _():
                pltpu.make_async_remote_copy(
                    src_ref=win.at[p],
                    dst_ref=trans.at[slab, :, half, :],
                    send_sem=win_send.at[p],
                    recv_sem=win_recv.at[slab, w % 2],
                    device_id=target,
                    device_id_type=MESH,
                ).start()

    @pl.when(slab < AHEAD)
    def _():
        hand_out()

    for p in range(4):
        target = member_at(slab, jnp.int32(p), tile // 16)

        @pl.when(same(target, me))
        def _():
            pltpu.make_async_copy(
                ints.at[p], int_in.at[tile % 16], int_recv.at[tile % 16]
            ).start()

        @pl.when(jnp.logical_not(same(target, me)))
        def _():
            pltpu.make_async_remote_copy(
                src_ref=ints.at[p],
                dst_ref=int_in.at[tile % 16],
                send_sem=int_send.at[p],
                recv_sem=int_recv.at[tile % 16],
                device_id=target,
                device_id_type=MESH,
            ).start()

    @pl.when((slab >= AHEAD) & jnp.logical_not(is_member))
    def _():
        pl.semaphore_wait(credit, 4)
        hand_out()

    def ask(s):
        @pl.when(slab == s)
        def _():
            hand_out()

        @pl.when((c_me % 2) * 2 + s // 4 != s % 4)
        def _():
            for j in range(2):
                pl.semaphore_signal(
                    credit,
                    1,
                    device_id=strip_at(band, s, 2 * c_me + j),
                    device_id_type=MESH,
                )

    def toeplitz(row, shift):
        lanes = jnp.broadcast_to(line[row : row + 1, :], (128, 256))
        return pltpu.roll(lanes, shift, 1, stride=1, stride_axis=0)

    def build(direction):
        plain, turned = (0, 8) if direction == 0 else (8, 0)
        sign = 1.0 if direction == 0 else -1.0
        real = toeplitz(plain, 224)
        imag = sign * toeplitz(plain + 1, 224)
        def rows(part):
            own = part[:, :128]
            return jnp.concatenate([own[:HALF], own[ROWS - HALF :]], axis=0), own[HALF : ROWS - HALF]

        (rim_real, core_real), (rim_imag, core_imag) = rows(real), rows(imag)
        for matrix, re_part, im_part in (
            (row_rim, rim_real, rim_imag),
            (row_core, core_real, core_imag),
        ):
            matrix[direction, :64, :128] = re_part.astype(BF16)
            matrix[direction, :64, 128:] = (-im_part).astype(BF16)
            matrix[direction, 64:, :128] = im_part.astype(BF16)
            matrix[direction, 64:, 128:] = re_part.astype(BF16)
        rim_re, rim_im = real[:, 128:], imag[:, 128:]
        lane = lax.broadcasted_iota(jnp.int32, (128, 128), 1)

        def weave(first, second):
            low = jnp.where(lane < 32, first, pltpu.roll(first, 64, 1))
            high = jnp.where(lane < 96, pltpu.roll(second, 64, 1), second)
            return jnp.where(lane < 64, low, high)

        def rim(part):
            return jnp.concatenate([part[:HALF], part[ROWS - HALF :]], axis=0).astype(BF16)

        row_halo[direction, :64, :] = rim(weave(rim_re, -rim_im))
        row_halo[direction, 64:, :] = rim(weave(rim_im, rim_re))
        for part in range(2):
            factor = 1.0 if part == 0 else sign
            far_part = factor * toeplitz(turned + part, 96)[:, :128]
            near_part = factor * toeplitz(turned + part, 224)[:, :128]
            columns = pl.ds(part * 128, 128)
            col_w[direction, :128, columns] = jnp.where(lane < 32, far_part, 0.0).astype(BF16)
            col_w[direction, 128:256, columns] = near_part.astype(BF16)
            col_w[direction, 256:, columns] = jnp.where(lane >= 96, far_part, 0.0).astype(BF16)

    def along_columns(field, direction):
        reals, imags = [], []
        for j in range(4):
            low, high = max(0, j - 1), min(4, j + 2)
            weights = col_w[direction, (low - j + 1) * 128 : (high - j + 1) * 128, :]
            both = dot(field[:, low * 128 : high * 128], weights)
            reals.append(both[:64, :128] - both[64:, 128:])
            imags.append(both[:64, 128:] + both[64:, :128])
        return jnp.concatenate(reals, axis=1), jnp.concatenate(imags, axis=1)

    top, middle, bottom = (
        pl.ds(0, HALF),
        pl.ds(HALF, ROWS - 2 * HALF),
        pl.ds(ROWS - HALF, HALF),
    )

    def get_rim(ref):
        return jnp.concatenate(
            [ref[part, rows, :] for part in range(2) for rows in (top, bottom)], axis=0
        )

    def put_rim(ref, real, imag):
        for part, value in ((0, real), (1, imag)):
            value = value.astype(BF16)
            ref[part, top, :] = value[:HALF]
            ref[part, bottom, :] = value[HALF:]

    def get_core(ref):
        return jnp.concatenate([ref[0, middle, :], ref[1, middle, :]], axis=0)

    def put_core(ref, real, imag):
        ref[0, middle, :] = real.astype(BF16)
        ref[1, middle, :] = imag.astype(BF16)

    def halo_copies(step, field):
        above = pltpu.make_async_remote_copy(
            src_ref=field.at[:, 0:HALF, :],
            dst_ref=halo.at[step, :, 0],
            send_sem=halo_send.at[step, 0],
            recv_sem=halo_recv.at[step, 0],
            device_id=member_at(band, p_me, (c_me + 3) % 4),
            device_id_type=MESH,
        )
        below = pltpu.make_async_remote_copy(
            src_ref=field.at[:, ROWS - HALF : ROWS, :],
            dst_ref=halo.at[step, :, 1],
            send_sem=halo_send.at[step, 1],
            recv_sem=halo_recv.at[step, 1],
            device_id=member_at(band, p_me, (c_me + 1) % 4),
            device_id_type=MESH,
        )
        return above, below

    def halo_start(step, field):
        above, below = halo_copies(step, field)

        @pl.when(c_me > 0)
        def _():
            above.start()

        @pl.when(c_me < 3)
        def _():
            below.start()

    def halo_wait(step, field, sends):
        above, below = halo_copies(step, field)

        @pl.when(c_me < 3)
        def _():
            if sends:
                below.wait_send()
            else:
                above.wait_recv()

        @pl.when(c_me > 0)
        def _():
            if sends:
                above.wait_send()
            else:
                below.wait_recv()

    def core_rows(field, direction):
        own = field[...].reshape(2 * ROWS, WIN)
        acc[...] = dot(row_rim[direction], own)
        return dot(row_core[direction], own)

    def rim_rows(step, field, direction):
        halo_wait(step, field, False)
        return acc[...] + dot(row_halo[direction], halo[step].reshape(4 * HALF, WIN))

    @pl.when(is_member)
    def _():
        tables = [
            pltpu.make_async_copy(cos_hbm, cos_t, table_sem.at[0]),
            pltpu.make_async_copy(sin_hbm, sin_t, table_sem.at[1]),
            pltpu.make_async_copy(
                probe.at[:, pl.ds(pl.multiple_of(c_me * ROWS, ROWS), ROWS), :],
                waves.at[0],
                table_sem.at[2],
            ),
        ]
        for copy in tables:
            copy.start()
        line[...] = jnp.zeros_like(line)
        line[0:2, 0 : 2 * HALF + 1] = taps[...].astype(F32)
        first = lax.broadcasted_iota(jnp.int32, (128, 128), 0)
        second = lax.broadcasted_iota(jnp.int32, (128, 128), 1)
        mirror = jnp.where(first + second == 2 * HALF, 1.0, 0.0).astype(BF16)
        line[8:, :128] = dot(line[:8, :128].astype(BF16), mirror)
        build(0)
        build(1)

        @pl.when(c_me == 0)
        def _():
            halo[:, :, 1] = jnp.zeros((16, 2, HALF, WIN), BF16)

        @pl.when(c_me == 3)
        def _():
            halo[:, :, 0] = jnp.zeros((16, 2, HALF, WIN), BF16)

        for copy in tables:
            copy.wait()

        def arrived(s):
            for j in range(2):
                part = trans.at[s, :, pl.ds(j * STRIP, STRIP), :]
                pltpu.make_async_copy(part, part, win_recv.at[s, j]).wait()

        def light(s, wave, get, put):
            wave_re, wave_im = wave
            both = get(trans.at[s]).astype(F32)
            trans_re, trans_im = both[:64], both[64:]
            put(
                lits.at[s],
                wave_re * trans_re - wave_im * trans_im,
                wave_re * trans_im + wave_im * trans_re,
            )

        def kept(s, get):
            both = get(waves.at[s]).astype(F32)
            return both[:64], both[64:]

        arrived(0)
        light(0, kept(0, get_rim), get_rim, put_rim)
        halo_start(0, lits.at[0])

        def forward(s, _):
            @pl.when(s + AHEAD < SLICES)
            def _():
                ask(s + AHEAD)

            light(s, kept(s, get_core), get_core, put_core)
            mid = core_rows(lits.at[s], 0).astype(BF16)
            put_core(waves.at[s + 1], *along_columns(mid, 0))

            @pl.when(s < SLICES - 1)
            def _():
                arrived(s + 1)

            mid = rim_rows(s, lits.at[s], 0).astype(BF16)
            put_rim(waves.at[s + 1], *along_columns(mid, 0))

            @pl.when(s < SLICES - 1)
            def _():
                light(s + 1, kept(s + 1, get_rim), get_rim, put_rim)
                halo_start(s + 1, lits.at[s + 1])

            return 0

        lax.fori_loop(0, SLICES, forward, 0)

        for i in range(16):
            pltpu.make_async_copy(int_in.at[i], int_in.at[i], int_recv.at[i]).wait()
        for part in range(2):
            values = int_in[:, part * 8 : part * 8 + 8, :].astype(F32).reshape(128, WIN // 2)
            int_t[part * (WIN // 2) : (part + 1) * (WIN // 2), :] = values.T

        exit_wave = waves[SLICES].reshape(2 * ROWS, WIN)
        by_cos, by_sin = dot(exit_wave, cos_t[...]), dot(exit_wave, sin_t[...])
        spec_re = ((by_cos[:128] + by_sin[128:]) * SCALE).astype(BF16)
        spec_im = ((by_cos[128:] - by_sin[:128]) * SCALE).astype(BF16)
        for k in range(4):
            stage[k, :, :128] = spec_re[:, k * 128 : (k + 1) * 128]
            stage[k, :, 128:] = spec_im[:, k * 128 : (k + 1) * 128]

        mine = pl.ds(pl.multiple_of(c_me * ROWS, ROWS), ROWS)

        def spec_copy(d):
            other = (c_me + d) % 4
            return pltpu.make_async_remote_copy(
                src_ref=stage.at[other],
                dst_ref=spec_in.at[mine, :],
                send_sem=spec_send.at[d],
                recv_sem=spec_recv.at[d],
                device_id=member_at(band, p_me, other),
                device_id_type=MESH,
            )

        for d in range(1, 4):
            spec_copy(d).start()
        spec_in[mine, :] = stage[c_me]
        for d in range(1, 4):
            spec_copy(d).wait()

        spectrum = spec_in[...]
        by_cos, by_sin = dot(cos_t[...], spectrum), dot(sin_t[...], spectrum)
        far_re = (by_cos[:, :128] + by_sin[:, 128:]) * SCALE
        far_im = (by_cos[:, 128:] - by_sin[:, :128]) * SCALE
        excess = far_re * far_re + far_im * far_im - int_t[...]
        err = jnp.concatenate(
            [(excess * far_re).astype(BF16), (excess * far_im).astype(BF16)], axis=1
        )
        by_cos, by_sin = dot(cos_t[...], err), dot(sin_t[...], err)
        back_re = ((by_cos[:, :128] - by_sin[:, 128:]) * SCALE).astype(BF16)
        back_im = ((by_cos[:, 128:] + by_sin[:, :128]) * SCALE).astype(BF16)
        for k in range(4):
            back_out[k, :, :128] = back_re[k * 128 : (k + 1) * 128]
            back_out[k, :, 128:] = back_im[k * 128 : (k + 1) * 128]

        def back_copy(d):
            other = (c_me + d) % 4
            return pltpu.make_async_remote_copy(
                src_ref=back_out.at[other],
                dst_ref=back_in.at[c_me],
                send_sem=back_send.at[d],
                recv_sem=back_recv.at[d],
                device_id=member_at(band, p_me, other),
                device_id_type=MESH,
            )

        for d in range(1, 4):
            back_copy(d).start()
        back_in[c_me] = back_out[c_me]
        for d in range(1, 4):
            back_copy(d).wait()

        back_all = jnp.concatenate(
            [
                jnp.concatenate([back_in[k, :, :128] for k in range(4)], axis=1),
                jnp.concatenate([back_in[k, :, 128:] for k in range(4)], axis=1),
            ],
            axis=0,
        )
        by_cos, by_sin = dot(back_all, cos_t[...]), dot(back_all, sin_t[...])
        gwave[0] = ((by_cos[:128] - by_sin[128:]) * SCALE).astype(BF16)
        gwave[1] = ((by_cos[128:] + by_sin[:128]) * SCALE).astype(BF16)

        def inc_target(s, j):
            return strip_at(band, s, 2 * c_me + j)

        def inc_copy(s, j):
            return pltpu.make_async_remote_copy(
                src_ref=incs.at[s, :, pl.ds(j * STRIP, STRIP), :],
                dst_ref=out.at[p_me],
                send_sem=inc_send.at[s, j],
                recv_sem=inc_recv.at[p_me],
                device_id=inc_target(s, j),
                device_id_type=MESH,
            )

        def inc_start(s):
            for j in range(2):
                local = same(inc_target(s, j), me)

                @pl.when(local)
                def _():
                    pltpu.make_async_copy(
                        incs.at[s, :, pl.ds(j * STRIP, STRIP), :], out.at[p_me], inc_recv.at[p_me]
                    ).start()

                @pl.when(jnp.logical_not(local))
                def _():
                    inc_copy(s, j).start()

        def increment(s, glit, get, put):
            seen_re, seen_im = kept(s, get)
            glit_re, glit_im = glit[:64], glit[64:]
            put(
                incs.at[s],
                glit_re * seen_re + glit_im * seen_im,
                glit_im * seen_re - glit_re * seen_im,
            )

        def pull(s, glit, get, put):
            both = get(trans.at[s]).astype(F32)
            trans_re, trans_im = both[:64], both[64:]
            glit_re, glit_im = glit[:64], glit[64:]
            put(
                gwave,
                trans_re * glit_re + trans_im * glit_im,
                trans_re * glit_im - trans_im * glit_re,
            )

        def send_rim(s):
            put_rim(gmids.at[s], *along_columns(get_rim(gwave), 1))
            halo_start(SLICES + s, gmids.at[s])

        send_rim(SLICES - 1)

        def backward(i, _):
            s = SLICES - 1 - i

            @pl.when(i > 0)
            def _():
                inc_start(s + 1)

            put_core(gmids.at[s], *along_columns(get_core(gwave), 1))
            glit = core_rows(gmids.at[s], 1)
            increment(s, glit, get_core, put_core)
            pull(s, glit, get_core, put_core)
            glit = rim_rows(SLICES + s, gmids.at[s], 1)
            pull(s, glit, get_rim, put_rim)

            @pl.when(s > 0)
            def _():
                send_rim(s - 1)

            increment(s, glit, get_rim, put_rim)
            return 0

        lax.fori_loop(0, SLICES, backward, 0)
        inc_start(0)

        def settle(s, _):
            halo_wait(s, lits.at[s], True)
            halo_wait(SLICES + s, gmids.at[s], True)
            for j in range(2):

                @pl.when(jnp.logical_not(same(inc_target(s, j), me)))
                def _():
                    inc_copy(s, j).wait_send()

            return 0

        lax.fori_loop(0, SLICES, settle, 0)

    for p in range(4):

        @pl.when(jnp.logical_not(same(member_at(band, jnp.int32(p), w // 2), me)))
        def _():
            pltpu.make_async_copy(win.at[p], win.at[p], win_send.at[p]).wait()

        @pl.when(jnp.logical_not(same(member_at(slab, jnp.int32(p), tile // 16), me)))
        def _():
            pltpu.make_async_copy(ints.at[p], ints.at[p], int_send.at[p]).wait()

        pltpu.make_async_copy(out.at[p], out.at[p], inc_recv.at[p]).wait()


def chain(win, ints, probe, taps):
    hbm = pl.BlockSpec(memory_space=pl.ANY)
    vmem = pl.BlockSpec(memory_space=pltpu.VMEM)
    cos_table, sin_table = (jnp.asarray(t, BF16) for t in fourier_tables())
    dma = pltpu.SemaphoreType.DMA
    group = (2, ROWS, WIN)
    return pl.pallas_call(
        chain_kernel,
        in_specs=[hbm, hbm, hbm, vmem, hbm, hbm],
        out_specs=hbm,
        out_shape=jax.ShapeDtypeStruct((4, 2, STRIP, WIN), BF16),
        scratch_shapes=[
            pltpu.VMEM((16, 256), F32),
            pltpu.VMEM((SLICES,) + group, BF16),
            pltpu.VMEM((SLICES + 1,) + group, BF16),
            pltpu.VMEM((SLICES,) + group, BF16),
            pltpu.VMEM((SLICES,) + group, BF16),
            pltpu.VMEM((SLICES,) + group, BF16),
            pltpu.VMEM((2 * SLICES, 2, 2, HALF, WIN), BF16),
            pltpu.VMEM((ROWS, WIN), F32),
            pltpu.VMEM(group, BF16),
            pltpu.VMEM((2, 128, 256), BF16),
            pltpu.VMEM((2, 128, 256), BF16),
            pltpu.VMEM((2, 128, 128), BF16),
            pltpu.VMEM((2, 384, 256), BF16),
            pltpu.VMEM((WIN, WIN), BF16),
            pltpu.VMEM((WIN, WIN), BF16),
            pltpu.VMEM((16, 16, WIN // 2), BF16),
            pltpu.VMEM((WIN, 128), F32),
            pltpu.VMEM((4, 128, 256), BF16),
            pltpu.VMEM((WIN, 256), BF16),
            pltpu.VMEM((4, 128, 256), BF16),
            pltpu.VMEM((4, 128, 256), BF16),
            pltpu.SemaphoreType.REGULAR,
            dma((4,)),
            dma((SLICES, 2)),
            dma((4,)),
            dma((16,)),
            dma((2 * SLICES, 2)),
            dma((2 * SLICES, 2)),
            dma((SLICES, 2)),
            dma((4,)),
            dma((4,)),
            dma((4,)),
            dma((4,)),
            dma((4,)),
            dma((3,)),
        ],
        compiler_params=pltpu.CompilerParams(
            collective_id=0, has_side_effects=True, vmem_limit_bytes=60 << 20
        ),
        name="chain",
    )(win, ints, probe, taps, cos_table, sin_table)


def on_device(phase, absorption, probe, taps, offsets, intensity):
    slab = lax.axis_index("slab")
    band = ((lax.axis_index("tile") + 60) % 64) // 8
    starts = lax.dynamic_slice_in_dim(offsets, band * 2, 2, 1).reshape(4)
    info = jnp.concatenate([starts, slab[None].astype(jnp.int32)])
    win, trans, ints = prepare(info, phase[0], absorption[0], intensity)
    inc = chain(win, ints, probe, taps)
    return finish(info, inc, trans)[None]


def solution(mesh):
    placed = (
        P("slab", "tile", None),
        P("slab", "tile", None),
        P(),
        P(),
        P(),
        P(None, "tile", None, None, None),
    )
    return jax.shard_map(
        on_device,
        mesh=mesh,
        in_specs=placed,
        out_specs=P("slab", None, "tile", None),
        check_vma=False,
    )
```

```python
import functools
import math

import jax
import jax.numpy as jnp
import numpy as np
from jax import lax
from jax.experimental import pallas as pl
from jax.experimental.pallas import tpu as pltpu
from jax.sharding import PartitionSpec as P

MESH = pl.DeviceIdType.MESH
F32 = jnp.float32
BF16 = jnp.bfloat16
WIN = 512
HALF = 32
NXO = 2048
SLICES = 8
STRIP = 64
AHEAD = 4
ROWS = 128
SCALE = WIN**-0.5


def dot(a, b):
    return jnp.dot(a, b, preferred_element_type=F32)


def fourier_tables():
    line = np.arange(WIN)
    angles = (line[:, None] * line[None, :] % WIN).astype(np.float64) * (2.0 * math.pi / WIN)
    return np.cos(angles).astype(np.float32), np.sin(angles).astype(np.float32)


def sincos(x):
    h = 0.5 * x
    q = h * h
    s = -2.50521084e-8
    for term in (2.75573192e-6, -1.98412698e-4, 8.33333333e-3, -1.66666667e-1, 1.0):
        s = s * q + term
    s = s * h
    c = 2.08767570e-9
    for term in (-2.75573192e-7, 2.48015873e-5, -1.38888889e-3, 4.16666667e-2, -0.5, 1.0):
        c = c * q + term
    return 2.0 * s * c, 1.0 - 2.0 * s * s


def finish_kernel(info, inc_hbm, trans_hbm, out, inc, trans, wide, sems):
    copies = [pltpu.make_async_copy(inc_hbm.at[p], inc.at[p], sems.at[p]) for p in range(4)]
    copies.append(pltpu.make_async_copy(trans_hbm, trans, sems.at[4]))
    for copy in copies:
        copy.start()
    wide[...] = jnp.zeros_like(wide)
    blank = jnp.zeros((STRIP, 128), F32)
    for p in range(4):
        copies[p].wait()
        start = info[p]
        base = pl.multiple_of(start // 128 * 128, 128)
        for part in range(2):
            block = jnp.concatenate([inc[p, part].astype(F32), blank], axis=1)
            wide[part, :, pl.ds(base, 640)] += pltpu.roll(block, start % 128, 1)
    copies[4].wait()
    real, imag = trans[0], trans[1]
    grad_re, grad_im = wide[0, :, :NXO], wide[1, :, :NXO]
    out[0] = grad_im * real - grad_re * imag
    out[1] = -(grad_re * real + grad_im * imag)


def finish(info, inc, trans):
    hbm = pl.BlockSpec(memory_space=pl.ANY)
    vmem = pl.BlockSpec(memory_space=pltpu.VMEM)
    return pl.pallas_call(
        finish_kernel,
        in_specs=[pl.BlockSpec(memory_space=pltpu.SMEM), hbm, hbm],
        out_specs=vmem,
        out_shape=jax.ShapeDtypeStruct((2, STRIP, NXO), F32),
        scratch_shapes=[
            pltpu.VMEM((4, 2, STRIP, WIN), BF16),
            pltpu.VMEM((2, STRIP, NXO), F32),
            pltpu.VMEM((2, STRIP, NXO + 128), F32),
            pltpu.SemaphoreType.DMA((5,)),
        ],
        compiler_params=pltpu.CompilerParams(vmem_limit_bytes=60 << 20),
        name="finish",
    )(info, inc, trans)


def device_at(x, y, z, core):
    return ((y % 2) * 4 + x, (z % 16) * 4 + (y // 2) * 2 + core)


def member_at(band, p, c):
    upper = c // 2
    return device_at(p, p, 2 * band + 1 + upper, (c + upper) % 2)


def strip_at(band, layer, w):
    return (layer, (band * 8 + 4 + w) % 64)


def same(a, b):
    return (a[0] == b[0]) & (a[1] == b[1])


def chain_kernel(
    info, phase_hbm, absorb_hbm, intensity_hbm, probe, taps, cos_hbm, sin_hbm, out, full_out,
    phase, absorb, intensity, full, win, ints, line, trans, waves, lits, gmids, incs, halo, acc, gwave,
    row_rim, row_core, row_halo, col_w, cos_t, sin_t, int_in, int_t,
    stage, spec_in, back_out, back_in,
    credit, win_send, win_recv, int_send, int_recv, halo_send, halo_recv,
    inc_send, inc_recv, spec_send, spec_recv, back_send, back_recv, table_sem, load_sem,
):
    slab = lax.axis_index("slab")
    tile = lax.axis_index("tile")
    me = (slab, tile)
    band = ((tile + 60) % 64) // 8
    w = (tile + 60) % 8
    x, y = slab % 4, (tile // 2) % 2 * 2 + slab // 4
    upper = w // 4
    is_member = y == x
    p_me = x
    c_me = upper * 2 + (tile % 2 + upper) % 2

    loads = [
        pltpu.make_async_copy(phase_hbm, phase, load_sem.at[0]),
        pltpu.make_async_copy(absorb_hbm, absorb, load_sem.at[1]),
        pltpu.make_async_copy(intensity_hbm.at[:, :, slab], intensity, load_sem.at[2]),
    ]
    for copy in loads:
        copy.start()

    def signal(device):
        pl.semaphore_signal(pltpu.get_barrier_semaphore(), 1, device_id=device, device_id_type=MESH)

    @pl.when(is_member)
    def _():
        def greet(i, _):
            signal(strip_at(band, i // 2, 2 * c_me + i % 2))
            signal((band, 16 * c_me + i))
            return 0

        lax.fori_loop(0, 16, greet, 0)
        for d in range(1, 4):
            signal(member_at(band, p_me, (c_me + d) % 4))

    for p in range(4):
        signal(member_at(band, jnp.int32(p), w // 2))

    for copy in loads:
        copy.wait()
    for part in range(4):
        rows = pl.ds(part * 16, 16)
        sin_part, cos_part = sincos(phase[rows, :])
        decay = jnp.exp(-absorb[rows, :])
        full[0, rows, :NXO] = decay * cos_part
        full[1, rows, :NXO] = decay * sin_part
    full[:, :, NXO:] = jnp.zeros((2, STRIP, 512), F32)
    for p in range(4):
        start = info[p]
        for part in range(2):
            block = full[part]
            for step, width in ((1024, 1536), (512, 1024), (256, 768), (128, 640)):
                shifted = jnp.full((STRIP, width), start) & step
                block = jnp.where(shifted > 0, block[:, step : step + width], block[:, :width])
            for step in (64, 32, 16, 8, 4, 2, 1):
                shifted = jnp.full((STRIP, 640), start) & step
                block = jnp.where(shifted > 0, pltpu.roll(block, 640 - step, 1), block)
            win[p, part] = block[:, :WIN].astype(BF16)
        values = intensity[p // 2, :, p % 2, :]
        halves = [values[:, : WIN // 2], values[:, WIN // 2 :]]
        ints[p] = jnp.concatenate(halves, axis=0).astype(BF16)
    full_copy = pltpu.make_async_copy(full.at[:, :, :NXO], full_out, load_sem.at[3])
    full_copy.start()
    barrier = pltpu.get_barrier_semaphore()

    @pl.when(is_member)
    def _():
        pl.semaphore_wait(barrier, 16 + 3 + 8)

    @pl.when(jnp.logical_not(is_member))
    def _():
        pl.semaphore_wait(barrier, 8)

    half = pl.ds(pl.multiple_of((w % 2) * STRIP, STRIP), STRIP)

    def hand_out():
        for p in range(4):
            target = member_at(band, jnp.int32(p), w // 2)

            @pl.when(same(target, me))
            def _():
                pltpu.make_async_copy(
                    win.at[p], trans.at[slab, :, half, :], win_recv.at[slab, w % 2]
                ).start()

            @pl.when(jnp.logical_not(same(target, me)))
            def _():
                pltpu.make_async_remote_copy(
                    src_ref=win.at[p],
                    dst_ref=trans.at[slab, :, half, :],
                    send_sem=win_send.at[p],
                    recv_sem=win_recv.at[slab, w % 2],
                    device_id=target,
                    device_id_type=MESH,
                ).start()

    @pl.when(slab < AHEAD)
    def _():
        hand_out()

    for p in range(4):
        target = member_at(slab, jnp.int32(p), tile // 16)

        @pl.when(same(target, me))
        def _():
            pltpu.make_async_copy(
                ints.at[p], int_in.at[tile % 16], int_recv.at[tile % 16]
            ).start()

        @pl.when(jnp.logical_not(same(target, me)))
        def _():
            pltpu.make_async_remote_copy(
                src_ref=ints.at[p],
                dst_ref=int_in.at[tile % 16],
                send_sem=int_send.at[p],
                recv_sem=int_recv.at[tile % 16],
                device_id=target,
                device_id_type=MESH,
            ).start()

    @pl.when((slab >= AHEAD) & jnp.logical_not(is_member))
    def _():
        pl.semaphore_wait(credit, 4)
        hand_out()

    def ask(s):
        @pl.when(slab == s)
        def _():
            hand_out()

        @pl.when((c_me % 2) * 2 + s // 4 != s % 4)
        def _():
            for j in range(2):
                pl.semaphore_signal(
                    credit,
                    1,
                    device_id=strip_at(band, s, 2 * c_me + j),
                    device_id_type=MESH,
                )

    def toeplitz(row, shift):
        lanes = jnp.broadcast_to(line[row : row + 1, :], (128, 256))
        return pltpu.roll(lanes, shift, 1, stride=1, stride_axis=0)

    def build(direction):
        plain, turned = (0, 8) if direction == 0 else (8, 0)
        sign = 1.0 if direction == 0 else -1.0
        real = toeplitz(plain, 224)
        imag = sign * toeplitz(plain + 1, 224)
        def rows(part):
            own = part[:, :128]
            return jnp.concatenate([own[:HALF], own[ROWS - HALF :]], axis=0), own[HALF : ROWS - HALF]

        (rim_real, core_real), (rim_imag, core_imag) = rows(real), rows(imag)
        for matrix, re_part, im_part in (
            (row_rim, rim_real, rim_imag),
            (row_core, core_real, core_imag),
        ):
            matrix[direction, :64, :128] = re_part.astype(BF16)
            matrix[direction, :64, 128:] = (-im_part).astype(BF16)
            matrix[direction, 64:, :128] = im_part.astype(BF16)
            matrix[direction, 64:, 128:] = re_part.astype(BF16)
        rim_re, rim_im = real[:, 128:], imag[:, 128:]
        lane = lax.broadcasted_iota(jnp.int32, (128, 128), 1)

        def weave(first, second):
            low = jnp.where(lane < 32, first, pltpu.roll(first, 64, 1))
            high = jnp.where(lane < 96, pltpu.roll(second, 64, 1), second)
            return jnp.where(lane < 64, low, high)

        def rim(part):
            return jnp.concatenate([part[:HALF], part[ROWS - HALF :]], axis=0).astype(BF16)

        row_halo[direction, :64, :] = rim(weave(rim_re, -rim_im))
        row_halo[direction, 64:, :] = rim(weave(rim_im, rim_re))
        for part in range(2):
            factor = 1.0 if part == 0 else sign
            far_part = factor * toeplitz(turned + part, 96)[:, :128]
            near_part = factor * toeplitz(turned + part, 224)[:, :128]
            columns = pl.ds(part * 128, 128)
            col_w[direction, :128, columns] = jnp.where(lane < 32, far_part, 0.0).astype(BF16)
            col_w[direction, 128:256, columns] = near_part.astype(BF16)
            col_w[direction, 256:, columns] = jnp.where(lane >= 96, far_part, 0.0).astype(BF16)

    def along_columns(field, direction):
        reals, imags = [], []
        for j in range(4):
            low, high = max(0, j - 1), min(4, j + 2)
            weights = col_w[direction, (low - j + 1) * 128 : (high - j + 1) * 128, :]
            both = dot(field[:, low * 128 : high * 128], weights)
            reals.append(both[:64, :128] - both[64:, 128:])
            imags.append(both[:64, 128:] + both[64:, :128])
        return jnp.concatenate(reals, axis=1), jnp.concatenate(imags, axis=1)

    top, middle, bottom = (
        pl.ds(0, HALF),
        pl.ds(HALF, ROWS - 2 * HALF),
        pl.ds(ROWS - HALF, HALF),
    )

    def get_rim(ref):
        return jnp.concatenate(
            [ref[part, rows, :] for part in range(2) for rows in (top, bottom)], axis=0
        )

    def put_rim(ref, real, imag):
        for part, value in ((0, real), (1, imag)):
            value = value.astype(BF16)
            ref[part, top, :] = value[:HALF]
            ref[part, bottom, :] = value[HALF:]

    def get_core(ref):
        return jnp.concatenate([ref[0, middle, :], ref[1, middle, :]], axis=0)

    def put_core(ref, real, imag):
        ref[0, middle, :] = real.astype(BF16)
        ref[1, middle, :] = imag.astype(BF16)

    def halo_copies(step, field):
        above = pltpu.make_async_remote_copy(
            src_ref=field.at[:, 0:HALF, :],
            dst_ref=halo.at[step, :, 0],
            send_sem=halo_send.at[step, 0],
            recv_sem=halo_recv.at[step, 0],
            device_id=member_at(band, p_me, (c_me + 3) % 4),
            device_id_type=MESH,
        )
        below = pltpu.make_async_remote_copy(
            src_ref=field.at[:, ROWS - HALF : ROWS, :],
            dst_ref=halo.at[step, :, 1],
            send_sem=halo_send.at[step, 1],
            recv_sem=halo_recv.at[step, 1],
            device_id=member_at(band, p_me, (c_me + 1) % 4),
            device_id_type=MESH,
        )
        return above, below

    def halo_start(step, field):
        above, below = halo_copies(step, field)

        @pl.when(c_me > 0)
        def _():
            above.start()

        @pl.when(c_me < 3)
        def _():
            below.start()

    def halo_wait(step, field, sends):
        above, below = halo_copies(step, field)

        @pl.when(c_me < 3)
        def _():
            if sends:
                below.wait_send()
            else:
                above.wait_recv()

        @pl.when(c_me > 0)
        def _():
            if sends:
                above.wait_send()
            else:
                below.wait_recv()

    def core_rows(field, direction):
        own = field[...].reshape(2 * ROWS, WIN)
        acc[...] = dot(row_rim[direction], own)
        return dot(row_core[direction], own)

    def rim_rows(step, field, direction):
        halo_wait(step, field, False)
        return acc[...] + dot(row_halo[direction], halo[step].reshape(4 * HALF, WIN))

    @pl.when(is_member)
    def _():
        tables = [
            pltpu.make_async_copy(cos_hbm, cos_t, table_sem.at[0]),
            pltpu.make_async_copy(sin_hbm, sin_t, table_sem.at[1]),
            pltpu.make_async_copy(
                probe.at[:, pl.ds(pl.multiple_of(c_me * ROWS, ROWS), ROWS), :],
                waves.at[0],
                table_sem.at[2],
            ),
        ]
        for copy in tables:
            copy.start()
        line[...] = jnp.zeros_like(line)
        line[0:2, 0 : 2 * HALF + 1] = taps[...].astype(F32)
        first = lax.broadcasted_iota(jnp.int32, (128, 128), 0)
        second = lax.broadcasted_iota(jnp.int32, (128, 128), 1)
        mirror = jnp.where(first + second == 2 * HALF, 1.0, 0.0).astype(BF16)
        line[8:, :128] = dot(line[:8, :128].astype(BF16), mirror)
        build(0)
        build(1)

        @pl.when(c_me == 0)
        def _():
            halo[:, :, 1] = jnp.zeros((16, 2, HALF, WIN), BF16)

        @pl.when(c_me == 3)
        def _():
            halo[:, :, 0] = jnp.zeros((16, 2, HALF, WIN), BF16)

        for copy in tables:
            copy.wait()

        def arrived(s):
            for j in range(2):
                part = trans.at[s, :, pl.ds(j * STRIP, STRIP), :]
                pltpu.make_async_copy(part, part, win_recv.at[s, j]).wait()

        def light(s, wave, get, put):
            wave_re, wave_im = wave
            both = get(trans.at[s]).astype(F32)
            trans_re, trans_im = both[:64], both[64:]
            put(
                lits.at[s],
                wave_re * trans_re - wave_im * trans_im,
                wave_re * trans_im + wave_im * trans_re,
            )

        def kept(s, get):
            both = get(waves.at[s]).astype(F32)
            return both[:64], both[64:]

        arrived(0)
        light(0, kept(0, get_rim), get_rim, put_rim)
        halo_start(0, lits.at[0])

        def forward(s, _):
            @pl.when(s + AHEAD < SLICES)
            def _():
                ask(s + AHEAD)

            light(s, kept(s, get_core), get_core, put_core)
            mid = core_rows(lits.at[s], 0).astype(BF16)
            put_core(waves.at[s + 1], *along_columns(mid, 0))

            @pl.when(s < SLICES - 1)
            def _():
                arrived(s + 1)

            mid = rim_rows(s, lits.at[s], 0).astype(BF16)
            put_rim(waves.at[s + 1], *along_columns(mid, 0))

            @pl.when(s < SLICES - 1)
            def _():
                light(s + 1, kept(s + 1, get_rim), get_rim, put_rim)
                halo_start(s + 1, lits.at[s + 1])

            return 0

        lax.fori_loop(0, SLICES, forward, 0)

        for i in range(16):
            pltpu.make_async_copy(int_in.at[i], int_in.at[i], int_recv.at[i]).wait()
        for part in range(2):
            values = int_in[:, part * 8 : part * 8 + 8, :].astype(F32).reshape(128, WIN // 2)
            int_t[part * (WIN // 2) : (part + 1) * (WIN // 2), :] = values.T

        exit_wave = waves[SLICES].reshape(2 * ROWS, WIN)
        by_cos, by_sin = dot(exit_wave, cos_t[...]), dot(exit_wave, sin_t[...])
        spec_re = ((by_cos[:128] + by_sin[128:]) * SCALE).astype(BF16)
        spec_im = ((by_cos[128:] - by_sin[:128]) * SCALE).astype(BF16)
        for k in range(4):
            stage[k, :, :128] = spec_re[:, k * 128 : (k + 1) * 128]
            stage[k, :, 128:] = spec_im[:, k * 128 : (k + 1) * 128]

        mine = pl.ds(pl.multiple_of(c_me * ROWS, ROWS), ROWS)

        def spec_copy(d):
            other = (c_me + d) % 4
            return pltpu.make_async_remote_copy(
                src_ref=stage.at[other],
                dst_ref=spec_in.at[mine, :],
                send_sem=spec_send.at[d],
                recv_sem=spec_recv.at[d],
                device_id=member_at(band, p_me, other),
                device_id_type=MESH,
            )

        for d in range(1, 4):
            spec_copy(d).start()
        spec_in[mine, :] = stage[c_me]
        for d in range(1, 4):
            spec_copy(d).wait()

        spectrum = spec_in[...]
        by_cos, by_sin = dot(cos_t[...], spectrum), dot(sin_t[...], spectrum)
        far_re = (by_cos[:, :128] + by_sin[:, 128:]) * SCALE
        far_im = (by_cos[:, 128:] - by_sin[:, :128]) * SCALE
        excess = far_re * far_re + far_im * far_im - int_t[...]
        err = jnp.concatenate(
            [(excess * far_re).astype(BF16), (excess * far_im).astype(BF16)], axis=1
        )
        by_cos, by_sin = dot(cos_t[...], err), dot(sin_t[...], err)
        back_re = ((by_cos[:, :128] - by_sin[:, 128:]) * SCALE).astype(BF16)
        back_im = ((by_cos[:, 128:] + by_sin[:, :128]) * SCALE).astype(BF16)
        for k in range(4):
            back_out[k, :, :128] = back_re[k * 128 : (k + 1) * 128]
            back_out[k, :, 128:] = back_im[k * 128 : (k + 1) * 128]

        def back_copy(d):
            other = (c_me + d) % 4
            return pltpu.make_async_remote_copy(
                src_ref=back_out.at[other],
                dst_ref=back_in.at[c_me],
                send_sem=back_send.at[d],
                recv_sem=back_recv.at[d],
                device_id=member_at(band, p_me, other),
                device_id_type=MESH,
            )

        for d in range(1, 4):
            back_copy(d).start()
        back_in[c_me] = back_out[c_me]
        for d in range(1, 4):
            back_copy(d).wait()

        back_all = jnp.concatenate(
            [
                jnp.concatenate([back_in[k, :, :128] for k in range(4)], axis=1),
                jnp.concatenate([back_in[k, :, 128:] for k in range(4)], axis=1),
            ],
            axis=0,
        )
        by_cos, by_sin = dot(back_all, cos_t[...]), dot(back_all, sin_t[...])
        gwave[0] = ((by_cos[:128] - by_sin[128:]) * SCALE).astype(BF16)
        gwave[1] = ((by_cos[128:] + by_sin[:128]) * SCALE).astype(BF16)

        def inc_target(s, j):
            return strip_at(band, s, 2 * c_me + j)

        def inc_copy(s, j):
            return pltpu.make_async_remote_copy(
                src_ref=incs.at[s, :, pl.ds(j * STRIP, STRIP), :],
                dst_ref=out.at[p_me],
                send_sem=inc_send.at[s, j],
                recv_sem=inc_recv.at[p_me],
                device_id=inc_target(s, j),
                device_id_type=MESH,
            )

        def inc_start(s):
            for j in range(2):
                local = same(inc_target(s, j), me)

                @pl.when(local)
                def _():
                    pltpu.make_async_copy(
                        incs.at[s, :, pl.ds(j * STRIP, STRIP), :], out.at[p_me], inc_recv.at[p_me]
                    ).start()

                @pl.when(jnp.logical_not(local))
                def _():
                    inc_copy(s, j).start()

        def increment(s, glit, get, put):
            seen_re, seen_im = kept(s, get)
            glit_re, glit_im = glit[:64], glit[64:]
            put(
                incs.at[s],
                glit_re * seen_re + glit_im * seen_im,
                glit_im * seen_re - glit_re * seen_im,
            )

        def pull(s, glit, get, put):
            both = get(trans.at[s]).astype(F32)
            trans_re, trans_im = both[:64], both[64:]
            glit_re, glit_im = glit[:64], glit[64:]
            put(
                gwave,
                trans_re * glit_re + trans_im * glit_im,
                trans_re * glit_im - trans_im * glit_re,
            )

        def send_rim(s):
            put_rim(gmids.at[s], *along_columns(get_rim(gwave), 1))
            halo_start(SLICES + s, gmids.at[s])

        send_rim(SLICES - 1)

        def backward(i, _):
            s = SLICES - 1 - i

            @pl.when(i > 0)
            def _():
                inc_start(s + 1)

            put_core(gmids.at[s], *along_columns(get_core(gwave), 1))
            glit = core_rows(gmids.at[s], 1)
            increment(s, glit, get_core, put_core)
            pull(s, glit, get_core, put_core)
            glit = rim_rows(SLICES + s, gmids.at[s], 1)
            pull(s, glit, get_rim, put_rim)

            @pl.when(s > 0)
            def _():
                send_rim(s - 1)

            increment(s, glit, get_rim, put_rim)
            return 0

        lax.fori_loop(0, SLICES, backward, 0)
        inc_start(0)

        def settle(s, _):
            halo_wait(s, lits.at[s], True)
            halo_wait(SLICES + s, gmids.at[s], True)
            for j in range(2):

                @pl.when(jnp.logical_not(same(inc_target(s, j), me)))
                def _():
                    inc_copy(s, j).wait_send()

            return 0

        lax.fori_loop(0, SLICES, settle, 0)

    for p in range(4):

        @pl.when(jnp.logical_not(same(member_at(band, jnp.int32(p), w // 2), me)))
        def _():
            pltpu.make_async_copy(win.at[p], win.at[p], win_send.at[p]).wait()

        @pl.when(jnp.logical_not(same(member_at(slab, jnp.int32(p), tile // 16), me)))
        def _():
            pltpu.make_async_copy(ints.at[p], ints.at[p], int_send.at[p]).wait()

        pltpu.make_async_copy(out.at[p], out.at[p], inc_recv.at[p]).wait()
    full_copy.wait()


def chain(info, phase, absorb, intensity, probe, taps):
    hbm = pl.BlockSpec(memory_space=pl.ANY)
    vmem = pl.BlockSpec(memory_space=pltpu.VMEM)
    cos_table, sin_table = (jnp.asarray(t, BF16) for t in fourier_tables())
    dma = pltpu.SemaphoreType.DMA
    group = (2, ROWS, WIN)
    return pl.pallas_call(
        chain_kernel,
        in_specs=[pl.BlockSpec(memory_space=pltpu.SMEM), hbm, hbm, hbm, hbm, vmem, hbm, hbm],
        out_specs=[hbm, hbm],
        out_shape=[
            jax.ShapeDtypeStruct((4, 2, STRIP, WIN), BF16),
            jax.ShapeDtypeStruct((2, STRIP, NXO), F32),
        ],
        scratch_shapes=[
            pltpu.VMEM((STRIP, NXO), F32),
            pltpu.VMEM((STRIP, NXO), F32),
            pltpu.VMEM((2, 8, 2, WIN), F32),
            pltpu.VMEM((2, STRIP, NXO + 512), F32),
            pltpu.VMEM((4, 2, STRIP, WIN), BF16),
            pltpu.VMEM((4, 16, WIN // 2), BF16),
            pltpu.VMEM((16, 256), F32),
            pltpu.VMEM((SLICES,) + group, BF16),
            pltpu.VMEM((SLICES + 1,) + group, BF16),
            pltpu.VMEM((SLICES,) + group, BF16),
            pltpu.VMEM((SLICES,) + group, BF16),
            pltpu.VMEM((SLICES,) + group, BF16),
            pltpu.VMEM((2 * SLICES, 2, 2, HALF, WIN), BF16),
            pltpu.VMEM((ROWS, WIN), F32),
            pltpu.VMEM(group, BF16),
            pltpu.VMEM((2, 128, 256), BF16),
            pltpu.VMEM((2, 128, 256), BF16),
            pltpu.VMEM((2, 128, 128), BF16),
            pltpu.VMEM((2, 384, 256), BF16),
            pltpu.VMEM((WIN, WIN), BF16),
            pltpu.VMEM((WIN, WIN), BF16),
            pltpu.VMEM((16, 16, WIN // 2), BF16),
            pltpu.VMEM((WIN, 128), F32),
            pltpu.VMEM((4, 128, 256), BF16),
            pltpu.VMEM((WIN, 256), BF16),
            pltpu.VMEM((4, 128, 256), BF16),
            pltpu.VMEM((4, 128, 256), BF16),
            pltpu.SemaphoreType.REGULAR,
            dma((4,)),
            dma((SLICES, 2)),
            dma((4,)),
            dma((16,)),
            dma((2 * SLICES, 2)),
            dma((2 * SLICES, 2)),
            dma((SLICES, 2)),
            dma((4,)),
            dma((4,)),
            dma((4,)),
            dma((4,)),
            dma((4,)),
            dma((3,)),
            dma((4,)),
        ],
        compiler_params=pltpu.CompilerParams(
            collective_id=0, has_side_effects=True, vmem_limit_bytes=60 << 20
        ),
        name="chain",
    )(info, phase, absorb, intensity, probe, taps, cos_table, sin_table)


def on_device(phase, absorption, probe, taps, offsets, intensity):
    band = ((lax.axis_index("tile") + 60) % 64) // 8
    info = lax.dynamic_slice_in_dim(offsets, band * 2, 2, 1).reshape(4)
    inc, trans = chain(info, phase[0], absorption[0], intensity, probe, taps)
    return finish(info, inc, trans)[None]


def solution(mesh):
    placed = (
        P("slab", "tile", None),
        P("slab", "tile", None),
        P(),
        P(),
        P(),
        P(None, "tile", None, None, None),
    )
    return jax.shard_map(
        on_device,
        mesh=mesh,
        in_specs=placed,
        out_specs=P("slab", None, "tile", None),
        check_vma=False,
    )
```

```python
import functools
import math

import jax
import jax.numpy as jnp
import numpy as np
from jax import lax
from jax.experimental import pallas as pl
from jax.experimental.pallas import tpu as pltpu
from jax.sharding import PartitionSpec as P

MESH = pl.DeviceIdType.MESH
F32 = jnp.float32
BF16 = jnp.bfloat16
WIN = 512
HALF = 32
NXO = 2048
SLICES = 8
STRIP = 64
AHEAD = 4
ROWS = 128
SCALE = WIN**-0.5


def dot(a, b):
    return jnp.dot(a, b, preferred_element_type=F32)


def fourier_tables():
    line = np.arange(WIN)
    angles = (line[:, None] * line[None, :] % WIN).astype(np.float64) * (2.0 * math.pi / WIN)
    return np.cos(angles).astype(np.float32), np.sin(angles).astype(np.float32)


def sincos(x):
    h = 0.5 * x
    q = h * h
    s = -2.50521084e-8
    for term in (2.75573192e-6, -1.98412698e-4, 8.33333333e-3, -1.66666667e-1, 1.0):
        s = s * q + term
    s = s * h
    c = 2.08767570e-9
    for term in (-2.75573192e-7, 2.48015873e-5, -1.38888889e-3, 4.16666667e-2, -0.5, 1.0):
        c = c * q + term
    return 2.0 * s * c, 1.0 - 2.0 * s * s


def finish_kernel(info, inc_hbm, trans_hbm, out, inc, trans, wide, sems):
    copies = [pltpu.make_async_copy(inc_hbm.at[p], inc.at[p], sems.at[p]) for p in range(4)]
    copies.append(pltpu.make_async_copy(trans_hbm, trans, sems.at[4]))
    for copy in copies:
        copy.start()
    wide[...] = jnp.zeros_like(wide)
    blank = jnp.zeros((STRIP, 128), F32)
    for p in range(4):
        copies[p].wait()
        start = info[p]
        base = pl.multiple_of(start // 128 * 128, 128)
        for part in range(2):
            block = jnp.concatenate([inc[p, part].astype(F32), blank], axis=1)
            wide[part, :, pl.ds(base, 640)] += pltpu.roll(block, start % 128, 1)
    copies[4].wait()
    real, imag = trans[0], trans[1]
    grad_re, grad_im = wide[0, :, :NXO], wide[1, :, :NXO]
    out[0] = grad_im * real - grad_re * imag
    out[1] = -(grad_re * real + grad_im * imag)


def finish(info, inc, trans):
    hbm = pl.BlockSpec(memory_space=pl.ANY)
    vmem = pl.BlockSpec(memory_space=pltpu.VMEM)
    return pl.pallas_call(
        finish_kernel,
        in_specs=[pl.BlockSpec(memory_space=pltpu.SMEM), hbm, hbm],
        out_specs=vmem,
        out_shape=jax.ShapeDtypeStruct((2, STRIP, NXO), F32),
        scratch_shapes=[
            pltpu.VMEM((4, 2, STRIP, WIN), BF16),
            pltpu.VMEM((2, STRIP, NXO), F32),
            pltpu.VMEM((2, STRIP, NXO + 128), F32),
            pltpu.SemaphoreType.DMA((5,)),
        ],
        compiler_params=pltpu.CompilerParams(vmem_limit_bytes=60 << 20),
        name="finish",
    )(info, inc, trans)


def device_at(x, y, z, core):
    return ((y % 2) * 4 + x, (z % 16) * 4 + (y // 2) * 2 + core)


def member_at(band, p, c):
    upper = c // 2
    return device_at(p, p, 2 * band + 1 + upper, (c + upper) % 2)


def strip_at(band, layer, w):
    return (layer, (band * 8 + 4 + w) % 64)


def same(a, b):
    return (a[0] == b[0]) & (a[1] == b[1])


def chain_kernel(
    info, phase_hbm, absorb_hbm, intensity_hbm, probe, taps, cos_hbm, sin_hbm, out, full_out,
    phase, absorb, intensity, full, win, ints, line, trans, waves, lits, gmids, incs, halo, acc, gwave,
    row_rim, row_core, row_halo, col_w, cos_t, sin_t, int_in, int_t,
    stage, spec_in, back_out, back_in,
    credit, win_send, win_recv, int_send, int_recv, halo_send, halo_recv,
    inc_send, inc_recv, spec_send, spec_recv, back_send, back_recv, table_sem, load_sem,
):
    slab = lax.axis_index("slab")
    tile = lax.axis_index("tile")
    me = (slab, tile)
    band = ((tile + 60) % 64) // 8
    w = (tile + 60) % 8
    x, y = slab % 4, (tile // 2) % 2 * 2 + slab // 4
    upper = w // 4
    is_member = y == x
    p_me = x
    c_me = upper * 2 + (tile % 2 + upper) % 2

    loads = [
        pltpu.make_async_copy(phase_hbm, phase, load_sem.at[0]),
        pltpu.make_async_copy(absorb_hbm, absorb, load_sem.at[1]),
        pltpu.make_async_copy(intensity_hbm.at[:, :, slab], intensity, load_sem.at[2]),
    ]
    for copy in loads:
        copy.start()

    def signal(device):
        pl.semaphore_signal(pltpu.get_barrier_semaphore(), 1, device_id=device, device_id_type=MESH)

    @pl.when(is_member)
    def _():
        def greet(i, _):
            signal(strip_at(band, i // 2, 2 * c_me + i % 2))
            signal((band, 16 * c_me + i))
            return 0

        lax.fori_loop(0, 16, greet, 0)
        for d in range(1, 4):
            signal(member_at(band, p_me, (c_me + d) % 4))

    for p in range(4):
        signal(member_at(band, jnp.int32(p), w // 2))

    for copy in loads:
        copy.wait()
    for part in range(4):
        rows = pl.ds(part * 16, 16)
        sin_part, cos_part = sincos(phase[rows, :])
        decay = jnp.exp(-absorb[rows, :])
        full[0, rows, :NXO] = decay * cos_part
        full[1, rows, :NXO] = decay * sin_part
    full[:, :, NXO:] = jnp.zeros((2, STRIP, 512), F32)
    for p in range(4):
        start = info[p]
        blocks = []
        for part in range(2):
            block = full[part]
            for step, width in ((1024, 1536), (512, 1024), (256, 768), (128, 640)):
                shifted = jnp.full((STRIP, width), start) & step
                block = jnp.where(shifted > 0, block[:, step : step + width], block[:, :width])
            blocks.append(block.astype(BF16))
        source = lax.broadcasted_iota(jnp.int32, (256, 128), 0)
        place = lax.broadcasted_iota(jnp.int32, (256, 128), 1)
        pick = jnp.where(source - place == (jnp.full((256, 128), start) & 127), 1.0, 0.0)
        both = jnp.concatenate(blocks, axis=0)
        tall = jnp.concatenate([both[:, j * 128 : j * 128 + 256] for j in range(4)], axis=0)
        cut = dot(tall, pick.astype(BF16)).astype(BF16)
        for j in range(4):
            for part in range(2):
                first = j * 128 + part * STRIP
                win[p, part, :, j * 128 : (j + 1) * 128] = cut[first : first + STRIP]
        values = intensity[p // 2, :, p % 2, :]
        halves = [values[:, : WIN // 2], values[:, WIN // 2 :]]
        ints[p] = jnp.concatenate(halves, axis=0).astype(BF16)
    full_copy = pltpu.make_async_copy(full.at[:, :, :NXO], full_out, load_sem.at[3])
    full_copy.start()
    barrier = pltpu.get_barrier_semaphore()

    @pl.when(is_member)
    def _():
        pl.semaphore_wait(barrier, 16 + 3 + 8)

    @pl.when(jnp.logical_not(is_member))
    def _():
        pl.semaphore_wait(barrier, 8)

    half = pl.ds(pl.multiple_of((w % 2) * STRIP, STRIP), STRIP)

    def hand_out():
        for p in range(4):
            target = member_at(band, jnp.int32(p), w // 2)

            @pl.when(same(target, me))
            def _():
                pltpu.make_async_copy(
                    win.at[p], trans.at[slab, :, half, :], win_recv.at[slab, w % 2]
                ).start()

            @pl.when(jnp.logical_not(same(target, me)))
            def _():
                pltpu.make_async_remote_copy(
                    src_ref=win.at[p],
                    dst_ref=trans.at[slab, :, half, :],
                    send_sem=win_send.at[p],
                    recv_sem=win_recv.at[slab, w % 2],
                    device_id=target,
                    device_id_type=MESH,
                ).start()

    @pl.when(slab < AHEAD)
    def _():
        hand_out()

    for p in range(4):
        target = member_at(slab, jnp.int32(p), tile // 16)

        @pl.when(same(target, me))
        def _():
            pltpu.make_async_copy(
                ints.at[p], int_in.at[tile % 16], int_recv.at[tile % 16]
            ).start()

        @pl.when(jnp.logical_not(same(target, me)))
        def _():
            pltpu.make_async_remote_copy(
                src_ref=ints.at[p],
                dst_ref=int_in.at[tile % 16],
                send_sem=int_send.at[p],
                recv_sem=int_recv.at[tile % 16],
                device_id=target,
                device_id_type=MESH,
            ).start()

    @pl.when((slab >= AHEAD) & jnp.logical_not(is_member))
    def _():
        pl.semaphore_wait(credit, 4)
        hand_out()

    def ask(s):
        @pl.when(slab == s)
        def _():
            hand_out()

        @pl.when((c_me % 2) * 2 + s // 4 != s % 4)
        def _():
            for j in range(2):
                pl.semaphore_signal(
                    credit,
                    1,
                    device_id=strip_at(band, s, 2 * c_me + j),
                    device_id_type=MESH,
                )

    def toeplitz(row, shift):
        lanes = jnp.broadcast_to(line[row : row + 1, :], (128, 256))
        return pltpu.roll(lanes, shift, 1, stride=1, stride_axis=0)

    def build(direction):
        plain, turned = (0, 8) if direction == 0 else (8, 0)
        sign = 1.0 if direction == 0 else -1.0
        real = toeplitz(plain, 224)
        imag = sign * toeplitz(plain + 1, 224)
        def rows(part):
            own = part[:, :128]
            return jnp.concatenate([own[:HALF], own[ROWS - HALF :]], axis=0), own[HALF : ROWS - HALF]

        (rim_real, core_real), (rim_imag, core_imag) = rows(real), rows(imag)
        for matrix, re_part, im_part in (
            (row_rim, rim_real, rim_imag),
            (row_core, core_real, core_imag),
        ):
            matrix[direction, :64, :128] = re_part.astype(BF16)
            matrix[direction, :64, 128:] = (-im_part).astype(BF16)
            matrix[direction, 64:, :128] = im_part.astype(BF16)
            matrix[direction, 64:, 128:] = re_part.astype(BF16)
        rim_re, rim_im = real[:, 128:], imag[:, 128:]
        lane = lax.broadcasted_iota(jnp.int32, (128, 128), 1)

        def weave(first, second):
            low = jnp.where(lane < 32, first, pltpu.roll(first, 64, 1))
            high = jnp.where(lane < 96, pltpu.roll(second, 64, 1), second)
            return jnp.where(lane < 64, low, high)

        def rim(part):
            return jnp.concatenate([part[:HALF], part[ROWS - HALF :]], axis=0).astype(BF16)

        row_halo[direction, :64, :] = rim(weave(rim_re, -rim_im))
        row_halo[direction, 64:, :] = rim(weave(rim_im, rim_re))
        for part in range(2):
            factor = 1.0 if part == 0 else sign
            far_part = factor * toeplitz(turned + part, 96)[:, :128]
            near_part = factor * toeplitz(turned + part, 224)[:, :128]
            columns = pl.ds(part * 128, 128)
            col_w[direction, :128, columns] = jnp.where(lane < 32, far_part, 0.0).astype(BF16)
            col_w[direction, 128:256, columns] = near_part.astype(BF16)
            col_w[direction, 256:, columns] = jnp.where(lane >= 96, far_part, 0.0).astype(BF16)

    def along_columns(field, direction):
        reals, imags = [], []
        for j in range(4):
            low, high = max(0, j - 1), min(4, j + 2)
            weights = col_w[direction, (low - j + 1) * 128 : (high - j + 1) * 128, :]
            both = dot(field[:, low * 128 : high * 128], weights)
            reals.append(both[:64, :128] - both[64:, 128:])
            imags.append(both[:64, 128:] + both[64:, :128])
        return jnp.concatenate(reals, axis=1), jnp.concatenate(imags, axis=1)

    top, middle, bottom = (
        pl.ds(0, HALF),
        pl.ds(HALF, ROWS - 2 * HALF),
        pl.ds(ROWS - HALF, HALF),
    )

    def get_rim(ref):
        return jnp.concatenate(
            [ref[part, rows, :] for part in range(2) for rows in (top, bottom)], axis=0
        )

    def put_rim(ref, real, imag):
        for part, value in ((0, real), (1, imag)):
            value = value.astype(BF16)
            ref[part, top, :] = value[:HALF]
            ref[part, bottom, :] = value[HALF:]

    def get_core(ref):
        return jnp.concatenate([ref[0, middle, :], ref[1, middle, :]], axis=0)

    def put_core(ref, real, imag):
        ref[0, middle, :] = real.astype(BF16)
        ref[1, middle, :] = imag.astype(BF16)

    def halo_copies(step, field):
        above = pltpu.make_async_remote_copy(
            src_ref=field.at[:, 0:HALF, :],
            dst_ref=halo.at[step, :, 0],
            send_sem=halo_send.at[step, 0],
            recv_sem=halo_recv.at[step, 0],
            device_id=member_at(band, p_me, (c_me + 3) % 4),
            device_id_type=MESH,
        )
        below = pltpu.make_async_remote_copy(
            src_ref=field.at[:, ROWS - HALF : ROWS, :],
            dst_ref=halo.at[step, :, 1],
            send_sem=halo_send.at[step, 1],
            recv_sem=halo_recv.at[step, 1],
            device_id=member_at(band, p_me, (c_me + 1) % 4),
            device_id_type=MESH,
        )
        return above, below

    def halo_start(step, field):
        above, below = halo_copies(step, field)

        @pl.when(c_me > 0)
        def _():
            above.start()

        @pl.when(c_me < 3)
        def _():
            below.start()

    def halo_wait(step, field, sends):
        above, below = halo_copies(step, field)

        @pl.when(c_me < 3)
        def _():
            if sends:
                below.wait_send()
            else:
                above.wait_recv()

        @pl.when(c_me > 0)
        def _():
            if sends:
                above.wait_send()
            else:
                below.wait_recv()

    def core_rows(field, direction):
        own = field[...].reshape(2 * ROWS, WIN)
        acc[...] = dot(row_rim[direction], own)
        return dot(row_core[direction], own)

    def rim_rows(step, field, direction):
        halo_wait(step, field, False)
        return acc[...] + dot(row_halo[direction], halo[step].reshape(4 * HALF, WIN))

    @pl.when(is_member)
    def _():
        tables = [
            pltpu.make_async_copy(cos_hbm, cos_t, table_sem.at[0]),
            pltpu.make_async_copy(sin_hbm, sin_t, table_sem.at[1]),
            pltpu.make_async_copy(
                probe.at[:, pl.ds(pl.multiple_of(c_me * ROWS, ROWS), ROWS), :],
                waves.at[0],
                table_sem.at[2],
            ),
        ]
        for copy in tables:
            copy.start()
        line[...] = jnp.zeros_like(line)
        line[0:2, 0 : 2 * HALF + 1] = taps[...].astype(F32)
        first = lax.broadcasted_iota(jnp.int32, (128, 128), 0)
        second = lax.broadcasted_iota(jnp.int32, (128, 128), 1)
        mirror = jnp.where(first + second == 2 * HALF, 1.0, 0.0).astype(BF16)
        line[8:, :128] = dot(line[:8, :128].astype(BF16), mirror)
        build(0)
        build(1)

        @pl.when(c_me == 0)
        def _():
            halo[:, :, 1] = jnp.zeros((16, 2, HALF, WIN), BF16)

        @pl.when(c_me == 3)
        def _():
            halo[:, :, 0] = jnp.zeros((16, 2, HALF, WIN), BF16)

        for copy in tables:
            copy.wait()

        def arrived(s):
            for j in range(2):
                part = trans.at[s, :, pl.ds(j * STRIP, STRIP), :]
                pltpu.make_async_copy(part, part, win_recv.at[s, j]).wait()

        def light(s, wave, get, put):
            wave_re, wave_im = wave
            both = get(trans.at[s]).astype(F32)
            trans_re, trans_im = both[:64], both[64:]
            put(
                lits.at[s],
                wave_re * trans_re - wave_im * trans_im,
                wave_re * trans_im + wave_im * trans_re,
            )

        def kept(s, get):
            both = get(waves.at[s]).astype(F32)
            return both[:64], both[64:]

        arrived(0)
        light(0, kept(0, get_rim), get_rim, put_rim)
        halo_start(0, lits.at[0])

        def forward(s, _):
            @pl.when(s + AHEAD < SLICES)
            def _():
                ask(s + AHEAD)

            light(s, kept(s, get_core), get_core, put_core)
            mid = core_rows(lits.at[s], 0).astype(BF16)
            put_core(waves.at[s + 1], *along_columns(mid, 0))

            @pl.when(s < SLICES - 1)
            def _():
                arrived(s + 1)

            mid = rim_rows(s, lits.at[s], 0).astype(BF16)
            put_rim(waves.at[s + 1], *along_columns(mid, 0))

            @pl.when(s < SLICES - 1)
            def _():
                light(s + 1, kept(s + 1, get_rim), get_rim, put_rim)
                halo_start(s + 1, lits.at[s + 1])

            return 0

        lax.fori_loop(0, SLICES, forward, 0)

        for i in range(16):
            pltpu.make_async_copy(int_in.at[i], int_in.at[i], int_recv.at[i]).wait()
        for part in range(2):
            values = int_in[:, part * 8 : part * 8 + 8, :].astype(F32).reshape(128, WIN // 2)
            int_t[part * (WIN // 2) : (part + 1) * (WIN // 2), :] = values.T

        exit_wave = waves[SLICES].reshape(2 * ROWS, WIN)
        by_cos, by_sin = dot(exit_wave, cos_t[...]), dot(exit_wave, sin_t[...])
        spec_re = ((by_cos[:128] + by_sin[128:]) * SCALE).astype(BF16)
        spec_im = ((by_cos[128:] - by_sin[:128]) * SCALE).astype(BF16)
        for k in range(4):
            stage[k, :, :128] = spec_re[:, k * 128 : (k + 1) * 128]
            stage[k, :, 128:] = spec_im[:, k * 128 : (k + 1) * 128]

        mine = pl.ds(pl.multiple_of(c_me * ROWS, ROWS), ROWS)

        def spec_copy(d):
            other = (c_me + d) % 4
            return pltpu.make_async_remote_copy(
                src_ref=stage.at[other],
                dst_ref=spec_in.at[mine, :],
                send_sem=spec_send.at[d],
                recv_sem=spec_recv.at[d],
                device_id=member_at(band, p_me, other),
                device_id_type=MESH,
            )

        for d in range(1, 4):
            spec_copy(d).start()
        spec_in[mine, :] = stage[c_me]
        for d in range(1, 4):
            spec_copy(d).wait()

        spectrum = spec_in[...]
        by_cos, by_sin = dot(cos_t[...], spectrum), dot(sin_t[...], spectrum)
        far_re = (by_cos[:, :128] + by_sin[:, 128:]) * SCALE
        far_im = (by_cos[:, 128:] - by_sin[:, :128]) * SCALE
        excess = far_re * far_re + far_im * far_im - int_t[...]
        err = jnp.concatenate(
            [(excess * far_re).astype(BF16), (excess * far_im).astype(BF16)], axis=1
        )
        by_cos, by_sin = dot(cos_t[...], err), dot(sin_t[...], err)
        back_re = ((by_cos[:, :128] - by_sin[:, 128:]) * SCALE).astype(BF16)
        back_im = ((by_cos[:, 128:] + by_sin[:, :128]) * SCALE).astype(BF16)
        for k in range(4):
            back_out[k, :, :128] = back_re[k * 128 : (k + 1) * 128]
            back_out[k, :, 128:] = back_im[k * 128 : (k + 1) * 128]

        def back_copy(d):
            other = (c_me + d) % 4
            return pltpu.make_async_remote_copy(
                src_ref=back_out.at[other],
                dst_ref=back_in.at[c_me],
                send_sem=back_send.at[d],
                recv_sem=back_recv.at[d],
                device_id=member_at(band, p_me, other),
                device_id_type=MESH,
            )

        for d in range(1, 4):
            back_copy(d).start()
        back_in[c_me] = back_out[c_me]
        for d in range(1, 4):
            back_copy(d).wait()

        back_all = jnp.concatenate(
            [
                jnp.concatenate([back_in[k, :, :128] for k in range(4)], axis=1),
                jnp.concatenate([back_in[k, :, 128:] for k in range(4)], axis=1),
            ],
            axis=0,
        )
        by_cos, by_sin = dot(back_all, cos_t[...]), dot(back_all, sin_t[...])
        gwave[0] = ((by_cos[:128] - by_sin[128:]) * SCALE).astype(BF16)
        gwave[1] = ((by_cos[128:] + by_sin[:128]) * SCALE).astype(BF16)

        def inc_target(s, j):
            return strip_at(band, s, 2 * c_me + j)

        def inc_copy(s, j):
            return pltpu.make_async_remote_copy(
                src_ref=incs.at[s, :, pl.ds(j * STRIP, STRIP), :],
                dst_ref=out.at[p_me],
                send_sem=inc_send.at[s, j],
                recv_sem=inc_recv.at[p_me],
                device_id=inc_target(s, j),
                device_id_type=MESH,
            )

        def inc_start(s):
            for j in range(2):
                local = same(inc_target(s, j), me)

                @pl.when(local)
                def _():
                    pltpu.make_async_copy(
                        incs.at[s, :, pl.ds(j * STRIP, STRIP), :], out.at[p_me], inc_recv.at[p_me]
                    ).start()

                @pl.when(jnp.logical_not(local))
                def _():
                    inc_copy(s, j).start()

        def increment(s, glit, get, put):
            seen_re, seen_im = kept(s, get)
            glit_re, glit_im = glit[:64], glit[64:]
            put(
                incs.at[s],
                glit_re * seen_re + glit_im * seen_im,
                glit_im * seen_re - glit_re * seen_im,
            )

        def pull(s, glit, get, put):
            both = get(trans.at[s]).astype(F32)
            trans_re, trans_im = both[:64], both[64:]
            glit_re, glit_im = glit[:64], glit[64:]
            put(
                gwave,
                trans_re * glit_re + trans_im * glit_im,
                trans_re * glit_im - trans_im * glit_re,
            )

        def send_rim(s):
            put_rim(gmids.at[s], *along_columns(get_rim(gwave), 1))
            halo_start(SLICES + s, gmids.at[s])

        send_rim(SLICES - 1)

        def backward(i, _):
            s = SLICES - 1 - i

            @pl.when(i > 0)
            def _():
                inc_start(s + 1)

            put_core(gmids.at[s], *along_columns(get_core(gwave), 1))
            glit = core_rows(gmids.at[s], 1)
            increment(s, glit, get_core, put_core)
            pull(s, glit, get_core, put_core)
            glit = rim_rows(SLICES + s, gmids.at[s], 1)
            pull(s, glit, get_rim, put_rim)

            @pl.when(s > 0)
            def _():
                send_rim(s - 1)

            increment(s, glit, get_rim, put_rim)
            return 0

        lax.fori_loop(0, SLICES, backward, 0)
        inc_start(0)

        def settle(s, _):
            halo_wait(s, lits.at[s], True)
            halo_wait(SLICES + s, gmids.at[s], True)
            for j in range(2):

                @pl.when(jnp.logical_not(same(inc_target(s, j), me)))
                def _():
                    inc_copy(s, j).wait_send()

            return 0

        lax.fori_loop(0, SLICES, settle, 0)

    for p in range(4):

        @pl.when(jnp.logical_not(same(member_at(band, jnp.int32(p), w // 2), me)))
        def _():
            pltpu.make_async_copy(win.at[p], win.at[p], win_send.at[p]).wait()

        @pl.when(jnp.logical_not(same(member_at(slab, jnp.int32(p), tile // 16), me)))
        def _():
            pltpu.make_async_copy(ints.at[p], ints.at[p], int_send.at[p]).wait()

        pltpu.make_async_copy(out.at[p], out.at[p], inc_recv.at[p]).wait()
    full_copy.wait()


def chain(info, phase, absorb, intensity, probe, taps):
    hbm = pl.BlockSpec(memory_space=pl.ANY)
    vmem = pl.BlockSpec(memory_space=pltpu.VMEM)
    cos_table, sin_table = (jnp.asarray(t, BF16) for t in fourier_tables())
    dma = pltpu.SemaphoreType.DMA
    group = (2, ROWS, WIN)
    return pl.pallas_call(
        chain_kernel,
        in_specs=[pl.BlockSpec(memory_space=pltpu.SMEM), hbm, hbm, hbm, hbm, vmem, hbm, hbm],
        out_specs=[hbm, hbm],
        out_shape=[
            jax.ShapeDtypeStruct((4, 2, STRIP, WIN), BF16),
            jax.ShapeDtypeStruct((2, STRIP, NXO), F32),
        ],
        scratch_shapes=[
            pltpu.VMEM((STRIP, NXO), F32),
            pltpu.VMEM((STRIP, NXO), F32),
            pltpu.VMEM((2, 8, 2, WIN), F32),
            pltpu.VMEM((2, STRIP, NXO + 512), F32),
            pltpu.VMEM((4, 2, STRIP, WIN), BF16),
            pltpu.VMEM((4, 16, WIN // 2), BF16),
            pltpu.VMEM((16, 256), F32),
            pltpu.VMEM((SLICES,) + group, BF16),
            pltpu.VMEM((SLICES + 1,) + group, BF16),
            pltpu.VMEM((SLICES,) + group, BF16),
            pltpu.VMEM((SLICES,) + group, BF16),
            pltpu.VMEM((SLICES,) + group, BF16),
            pltpu.VMEM((2 * SLICES, 2, 2, HALF, WIN), BF16),
            pltpu.VMEM((ROWS, WIN), F32),
            pltpu.VMEM(group, BF16),
            pltpu.VMEM((2, 128, 256), BF16),
            pltpu.VMEM((2, 128, 256), BF16),
            pltpu.VMEM((2, 128, 128), BF16),
            pltpu.VMEM((2, 384, 256), BF16),
            pltpu.VMEM((WIN, WIN), BF16),
            pltpu.VMEM((WIN, WIN), BF16),
            pltpu.VMEM((16, 16, WIN // 2), BF16),
            pltpu.VMEM((WIN, 128), F32),
            pltpu.VMEM((4, 128, 256), BF16),
            pltpu.VMEM((WIN, 256), BF16),
            pltpu.VMEM((4, 128, 256), BF16),
            pltpu.VMEM((4, 128, 256), BF16),
            pltpu.SemaphoreType.REGULAR,
            dma((4,)),
            dma((SLICES, 2)),
            dma((4,)),
            dma((16,)),
            dma((2 * SLICES, 2)),
            dma((2 * SLICES, 2)),
            dma((SLICES, 2)),
            dma((4,)),
            dma((4,)),
            dma((4,)),
            dma((4,)),
            dma((4,)),
            dma((3,)),
            dma((4,)),
        ],
        compiler_params=pltpu.CompilerParams(
            collective_id=0, has_side_effects=True, vmem_limit_bytes=60 << 20
        ),
        name="chain",
    )(info, phase, absorb, intensity, probe, taps, cos_table, sin_table)


def on_device(phase, absorption, probe, taps, offsets, intensity):
    band = ((lax.axis_index("tile") + 60) % 64) // 8
    info = lax.dynamic_slice_in_dim(offsets, band * 2, 2, 1).reshape(4)
    inc, trans = chain(info, phase[0], absorption[0], intensity, probe, taps)
    return finish(info, inc, trans)[None]


def solution(mesh):
    placed = (
        P("slab", "tile", None),
        P("slab", "tile", None),
        P(),
        P(),
        P(),
        P(None, "tile", None, None, None),
    )
    return jax.shard_map(
        on_device,
        mesh=mesh,
        in_specs=placed,
        out_specs=P("slab", None, "tile", None),
        check_vma=False,
    )
```

```python
import functools
import math

import jax
import jax.numpy as jnp
import numpy as np
from jax import lax
from jax.experimental import pallas as pl
from jax.experimental.pallas import tpu as pltpu
from jax.sharding import PartitionSpec as P

MESH = pl.DeviceIdType.MESH
F32 = jnp.float32
BF16 = jnp.bfloat16
WIN = 512
HALF = 32
NXO = 2048
SLICES = 8
STRIP = 64
AHEAD = 4
ROWS = 128
SCALE = WIN**-0.5


def dot(a, b):
    return jnp.dot(a, b, preferred_element_type=F32)


def fourier_tables():
    line = np.arange(WIN)
    angles = (line[:, None] * line[None, :] % WIN).astype(np.float64) * (2.0 * math.pi / WIN)
    return np.cos(angles).astype(np.float32), np.sin(angles).astype(np.float32)


def sincos(x):
    h = 0.5 * x
    q = h * h
    s = -2.50521084e-8
    for term in (2.75573192e-6, -1.98412698e-4, 8.33333333e-3, -1.66666667e-1, 1.0):
        s = s * q + term
    s = s * h
    c = 2.08767570e-9
    for term in (-2.75573192e-7, 2.48015873e-5, -1.38888889e-3, 4.16666667e-2, -0.5, 1.0):
        c = c * q + term
    return 2.0 * s * c, 1.0 - 2.0 * s * s


def finish_kernel(info, inc_hbm, trans_hbm, out, inc, trans, wide, sems):
    copies = [pltpu.make_async_copy(inc_hbm.at[p], inc.at[p], sems.at[p]) for p in range(4)]
    copies.append(pltpu.make_async_copy(trans_hbm, trans, sems.at[4]))
    for copy in copies:
        copy.start()
    wide[...] = jnp.zeros_like(wide)
    blank = jnp.zeros((STRIP, 128), F32)
    for p in range(4):
        copies[p].wait()
        start = info[p]
        base = pl.multiple_of(start // 128 * 128, 128)
        for part in range(2):
            block = jnp.concatenate([inc[p, part].astype(F32), blank], axis=1)
            wide[part, :, pl.ds(base, 640)] += pltpu.roll(block, start % 128, 1)
    copies[4].wait()
    real, imag = trans[0], trans[1]
    grad_re, grad_im = wide[0, :, :NXO], wide[1, :, :NXO]
    out[0] = grad_im * real - grad_re * imag
    out[1] = -(grad_re * real + grad_im * imag)


def finish(info, inc, trans):
    hbm = pl.BlockSpec(memory_space=pl.ANY)
    vmem = pl.BlockSpec(memory_space=pltpu.VMEM)
    return pl.pallas_call(
        finish_kernel,
        in_specs=[pl.BlockSpec(memory_space=pltpu.SMEM), hbm, hbm],
        out_specs=vmem,
        out_shape=jax.ShapeDtypeStruct((2, STRIP, NXO), F32),
        scratch_shapes=[
            pltpu.VMEM((4, 2, STRIP, WIN), BF16),
            pltpu.VMEM((2, STRIP, NXO), F32),
            pltpu.VMEM((2, STRIP, NXO + 128), F32),
            pltpu.SemaphoreType.DMA((5,)),
        ],
        compiler_params=pltpu.CompilerParams(vmem_limit_bytes=60 << 20),
        name="finish",
    )(info, inc, trans)


def device_at(x, y, z, core):
    return ((y % 2) * 4 + x, (z % 16) * 4 + (y // 2) * 2 + core)


def member_at(band, p, c):
    upper = c // 2
    return device_at(p, p, 2 * band + 1 + upper, (c + upper) % 2)


def strip_at(band, layer, w):
    return (layer, (band * 8 + 4 + w) % 64)


def same(a, b):
    return (a[0] == b[0]) & (a[1] == b[1])


def chain_kernel(
    info, phase_hbm, absorb_hbm, intensity_hbm, probe, taps, cos_hbm, sin_hbm, out, full_out,
    phase, absorb, intensity, full, win, ints, line, trans, waves, lits, gmids, incs, halo, acc, gwave,
    row_rim, row_core, row_halo, col_w, cos_t, sin_t, int_in, int_t,
    stage, spec_in, back_out, back_in,
    credit, win_send, win_recv, int_send, int_recv, halo_send, halo_recv,
    inc_send, inc_recv, spec_send, spec_recv, back_send, back_recv, table_sem, load_sem,
):
    slab = lax.axis_index("slab")
    tile = lax.axis_index("tile")
    me = (slab, tile)
    band = ((tile + 60) % 64) // 8
    w = (tile + 60) % 8
    x, y = slab % 4, (tile // 2) % 2 * 2 + slab // 4
    upper = w // 4
    is_member = y == x
    p_me = x
    c_me = upper * 2 + (tile % 2 + upper) % 2

    loads = [
        pltpu.make_async_copy(phase_hbm, phase, load_sem.at[0]),
        pltpu.make_async_copy(absorb_hbm, absorb, load_sem.at[1]),
        pltpu.make_async_copy(intensity_hbm.at[:, :, slab], intensity, load_sem.at[2]),
    ]
    for copy in loads:
        copy.start()

    def signal(device):
        pl.semaphore_signal(pltpu.get_barrier_semaphore(), 1, device_id=device, device_id_type=MESH)

    @pl.when(is_member)
    def _():
        def greet(i, _):
            signal(strip_at(band, i // 2, 2 * c_me + i % 2))
            signal((band, 16 * c_me + i))
            return 0

        lax.fori_loop(0, 16, greet, 0)
        for d in range(1, 4):
            signal(member_at(band, p_me, (c_me + d) % 4))

    for p in range(4):
        signal(member_at(band, jnp.int32(p), w // 2))

    for copy in loads:
        copy.wait()
    for part in range(4):
        rows = pl.ds(part * 16, 16)
        sin_part, cos_part = sincos(phase[rows, :])
        decay = jnp.exp(-absorb[rows, :])
        full[0, rows, :NXO] = decay * cos_part
        full[1, rows, :NXO] = decay * sin_part
    full[:, :, NXO:] = jnp.zeros((2, STRIP, 512), F32)
    for p in range(4):
        start = info[p]
        blocks = []
        for part in range(2):
            block = full[part]
            for step, width in ((1024, 1536), (512, 1024), (256, 768), (128, 640)):
                shifted = jnp.full((STRIP, width), start) & step
                block = jnp.where(shifted > 0, block[:, step : step + width], block[:, :width])
            blocks.append(block.astype(BF16))
        source = lax.broadcasted_iota(jnp.int32, (256, 128), 0)
        place = lax.broadcasted_iota(jnp.int32, (256, 128), 1)
        pick = jnp.where(source - place == (jnp.full((256, 128), start) & 127), 1.0, 0.0)
        both = jnp.concatenate(blocks, axis=0)
        tall = jnp.concatenate([both[:, j * 128 : j * 128 + 256] for j in range(4)], axis=0)
        cut = dot(tall, pick.astype(BF16)).astype(BF16)
        for j in range(4):
            for part in range(2):
                first = j * 128 + part * STRIP
                win[p, part, :, j * 128 : (j + 1) * 128] = cut[first : first + STRIP]
        values = intensity[p // 2, :, p % 2, :]
        halves = [values[:, : WIN // 2], values[:, WIN // 2 :]]
        ints[p] = jnp.concatenate(halves, axis=0).astype(BF16)
    full_copy = pltpu.make_async_copy(full.at[:, :, :NXO], full_out, load_sem.at[3])
    full_copy.start()
    barrier = pltpu.get_barrier_semaphore()

    @pl.when(is_member)
    def _():
        pl.semaphore_wait(barrier, 16 + 3 + 8)

    @pl.when(jnp.logical_not(is_member))
    def _():
        pl.semaphore_wait(barrier, 8)

    half = pl.ds(pl.multiple_of((w % 2) * STRIP, STRIP), STRIP)

    def hand_out():
        for p in range(4):
            target = member_at(band, jnp.int32(p), w // 2)

            @pl.when(same(target, me))
            def _():
                pltpu.make_async_copy(
                    win.at[p], trans.at[slab, :, half, :], win_recv.at[slab, w % 2]
                ).start()

            @pl.when(jnp.logical_not(same(target, me)))
            def _():
                pltpu.make_async_remote_copy(
                    src_ref=win.at[p],
                    dst_ref=trans.at[slab, :, half, :],
                    send_sem=win_send.at[p],
                    recv_sem=win_recv.at[slab, w % 2],
                    device_id=target,
                    device_id_type=MESH,
                ).start()

    @pl.when(slab < AHEAD)
    def _():
        hand_out()

    for p in range(4):
        target = member_at(slab, jnp.int32(p), tile // 16)

        @pl.when(same(target, me))
        def _():
            pltpu.make_async_copy(
                ints.at[p], int_in.at[tile % 16], int_recv.at[tile % 16]
            ).start()

        @pl.when(jnp.logical_not(same(target, me)))
        def _():
            pltpu.make_async_remote_copy(
                src_ref=ints.at[p],
                dst_ref=int_in.at[tile % 16],
                send_sem=int_send.at[p],
                recv_sem=int_recv.at[tile % 16],
                device_id=target,
                device_id_type=MESH,
            ).start()

    @pl.when((slab >= AHEAD) & jnp.logical_not(is_member))
    def _():
        pl.semaphore_wait(credit, 4)
        hand_out()

    def ask(s):
        @pl.when(slab == s)
        def _():
            hand_out()

        @pl.when((c_me % 2) * 2 + s // 4 != s % 4)
        def _():
            for j in range(2):
                pl.semaphore_signal(
                    credit,
                    1,
                    device_id=strip_at(band, s, 2 * c_me + j),
                    device_id_type=MESH,
                )

    def toeplitz(row, shift):
        lanes = jnp.broadcast_to(line[row : row + 1, :], (128, 256))
        return pltpu.roll(lanes, shift, 1, stride=1, stride_axis=0)

    def build(direction):
        plain, turned = (0, 8) if direction == 0 else (8, 0)
        sign = 1.0 if direction == 0 else -1.0
        real = toeplitz(plain, 224)
        imag = sign * toeplitz(plain + 1, 224)
        def rows(part):
            own = part[:, :128]
            return jnp.concatenate([own[:HALF], own[ROWS - HALF :]], axis=0), own[HALF : ROWS - HALF]

        (rim_real, core_real), (rim_imag, core_imag) = rows(real), rows(imag)
        for matrix, re_part, im_part in (
            (row_rim, rim_real, rim_imag),
            (row_core, core_real, core_imag),
        ):
            matrix[direction, :64, :128] = re_part.astype(BF16)
            matrix[direction, :64, 128:] = (-im_part).astype(BF16)
            matrix[direction, 64:, :128] = im_part.astype(BF16)
            matrix[direction, 64:, 128:] = re_part.astype(BF16)
        rim_re, rim_im = real[:, 128:], imag[:, 128:]
        lane = lax.broadcasted_iota(jnp.int32, (128, 128), 1)

        def weave(first, second):
            low = jnp.where(lane < 32, first, pltpu.roll(first, 64, 1))
            high = jnp.where(lane < 96, pltpu.roll(second, 64, 1), second)
            return jnp.where(lane < 64, low, high)

        def rim(part):
            return jnp.concatenate([part[:HALF], part[ROWS - HALF :]], axis=0).astype(BF16)

        row_halo[direction, :64, :] = rim(weave(rim_re, -rim_im))
        row_halo[direction, 64:, :] = rim(weave(rim_im, rim_re))
        for part in range(2):
            factor = 1.0 if part == 0 else sign
            far_part = factor * toeplitz(turned + part, 96)[:, :128]
            near_part = factor * toeplitz(turned + part, 224)[:, :128]
            columns = pl.ds(part * 128, 128)
            col_w[direction, :128, columns] = jnp.where(lane < 32, far_part, 0.0).astype(BF16)
            col_w[direction, 128:256, columns] = near_part.astype(BF16)
            col_w[direction, 256:, columns] = jnp.where(lane >= 96, far_part, 0.0).astype(BF16)

    def along_columns(field, direction):
        reals, imags = [], []
        for j in range(4):
            low, high = max(0, j - 1), min(4, j + 2)
            weights = col_w[direction, (low - j + 1) * 128 : (high - j + 1) * 128, :]
            both = dot(field[:, low * 128 : high * 128], weights)
            reals.append(both[:64, :128] - both[64:, 128:])
            imags.append(both[:64, 128:] + both[64:, :128])
        return jnp.concatenate(reals, axis=1), jnp.concatenate(imags, axis=1)

    top, middle, bottom = (
        pl.ds(0, HALF),
        pl.ds(HALF, ROWS - 2 * HALF),
        pl.ds(ROWS - HALF, HALF),
    )

    def get_rim(ref):
        return jnp.concatenate(
            [ref[part, rows, :] for part in range(2) for rows in (top, bottom)], axis=0
        )

    def put_rim(ref, real, imag):
        for part, value in ((0, real), (1, imag)):
            value = value.astype(BF16)
            ref[part, top, :] = value[:HALF]
            ref[part, bottom, :] = value[HALF:]

    def get_core(ref):
        return jnp.concatenate([ref[0, middle, :], ref[1, middle, :]], axis=0)

    def put_core(ref, real, imag):
        ref[0, middle, :] = real.astype(BF16)
        ref[1, middle, :] = imag.astype(BF16)

    def halo_copies(step, field):
        above = pltpu.make_async_remote_copy(
            src_ref=field.at[:, 0:HALF, :],
            dst_ref=halo.at[step, :, 0],
            send_sem=halo_send.at[step, 0],
            recv_sem=halo_recv.at[step, 0],
            device_id=member_at(band, p_me, (c_me + 3) % 4),
            device_id_type=MESH,
        )
        below = pltpu.make_async_remote_copy(
            src_ref=field.at[:, ROWS - HALF : ROWS, :],
            dst_ref=halo.at[step, :, 1],
            send_sem=halo_send.at[step, 1],
            recv_sem=halo_recv.at[step, 1],
            device_id=member_at(band, p_me, (c_me + 1) % 4),
            device_id_type=MESH,
        )
        return above, below

    def halo_start(step, field):
        above, below = halo_copies(step, field)

        @pl.when(c_me > 0)
        def _():
            above.start()

        @pl.when(c_me < 3)
        def _():
            below.start()

    def halo_wait(step, field, sends):
        above, below = halo_copies(step, field)

        @pl.when(c_me < 3)
        def _():
            if sends:
                below.wait_send()
            else:
                above.wait_recv()

        @pl.when(c_me > 0)
        def _():
            if sends:
                above.wait_send()
            else:
                below.wait_recv()

    def core_rows(field, direction):
        own = field[...].reshape(2 * ROWS, WIN)
        acc[...] = dot(row_rim[direction], own)
        return dot(row_core[direction], own)

    def rim_rows(step, field, direction):
        halo_wait(step, field, False)
        return acc[...] + dot(row_halo[direction], halo[step].reshape(4 * HALF, WIN))

    @pl.when(is_member)
    def _():
        tables = [
            pltpu.make_async_copy(cos_hbm, cos_t, table_sem.at[0]),
            pltpu.make_async_copy(sin_hbm, sin_t, table_sem.at[1]),
            pltpu.make_async_copy(
                probe.at[:, pl.ds(pl.multiple_of(c_me * ROWS, ROWS), ROWS), :],
                waves.at[0],
                table_sem.at[2],
            ),
        ]
        for copy in tables:
            copy.start()
        line[...] = jnp.zeros_like(line)
        line[0:2, 0 : 2 * HALF + 1] = taps[...].astype(F32)
        first = lax.broadcasted_iota(jnp.int32, (128, 128), 0)
        second = lax.broadcasted_iota(jnp.int32, (128, 128), 1)
        mirror = jnp.where(first + second == 2 * HALF, 1.0, 0.0).astype(BF16)
        line[8:, :128] = dot(line[:8, :128].astype(BF16), mirror)
        build(0)
        build(1)

        @pl.when(c_me == 0)
        def _():
            halo[:, :, 1] = jnp.zeros((16, 2, HALF, WIN), BF16)

        @pl.when(c_me == 3)
        def _():
            halo[:, :, 0] = jnp.zeros((16, 2, HALF, WIN), BF16)

        for copy in tables:
            copy.wait()

        def arrived(s):
            for j in range(2):
                part = trans.at[s, :, pl.ds(j * STRIP, STRIP), :]
                pltpu.make_async_copy(part, part, win_recv.at[s, j]).wait()

        def light(s, wave, get, put):
            wave_re, wave_im = wave
            both = get(trans.at[s]).astype(F32)
            trans_re, trans_im = both[:64], both[64:]
            put(
                lits.at[s],
                wave_re * trans_re - wave_im * trans_im,
                wave_re * trans_im + wave_im * trans_re,
            )

        def kept(s, get):
            both = get(waves.at[s]).astype(F32)
            return both[:64], both[64:]

        arrived(0)
        light(0, kept(0, get_rim), get_rim, put_rim)
        halo_start(0, lits.at[0])

        def forward(s, _):
            @pl.when(s + AHEAD < SLICES)
            def _():
                ask(s + AHEAD)

            light(s, kept(s, get_core), get_core, put_core)
            mid = core_rows(lits.at[s], 0).astype(BF16)
            put_core(waves.at[s + 1], *along_columns(mid, 0))

            @pl.when(s < SLICES - 1)
            def _():
                arrived(s + 1)

            mid = rim_rows(s, lits.at[s], 0).astype(BF16)
            real, imag = (value.astype(BF16) for value in along_columns(mid, 0))

            @pl.when(s < SLICES - 1)
            def _():
                light(s + 1, (real.astype(F32), imag.astype(F32)), get_rim, put_rim)
                halo_start(s + 1, lits.at[s + 1])

            put_rim(waves.at[s + 1], real, imag)
            return 0

        lax.fori_loop(0, SLICES, forward, 0)

        for i in range(16):
            pltpu.make_async_copy(int_in.at[i], int_in.at[i], int_recv.at[i]).wait()
        for part in range(2):
            values = int_in[:, part * 8 : part * 8 + 8, :].astype(F32).reshape(128, WIN // 2)
            int_t[part * (WIN // 2) : (part + 1) * (WIN // 2), :] = values.T

        exit_wave = waves[SLICES].reshape(2 * ROWS, WIN)
        by_cos, by_sin = dot(exit_wave, cos_t[...]), dot(exit_wave, sin_t[...])
        spec_re = ((by_cos[:128] + by_sin[128:]) * SCALE).astype(BF16)
        spec_im = ((by_cos[128:] - by_sin[:128]) * SCALE).astype(BF16)
        for k in range(4):
            stage[k, :, :128] = spec_re[:, k * 128 : (k + 1) * 128]
            stage[k, :, 128:] = spec_im[:, k * 128 : (k + 1) * 128]

        mine = pl.ds(pl.multiple_of(c_me * ROWS, ROWS), ROWS)

        def spec_copy(d):
            other = (c_me + d) % 4
            return pltpu.make_async_remote_copy(
                src_ref=stage.at[other],
                dst_ref=spec_in.at[mine, :],
                send_sem=spec_send.at[d],
                recv_sem=spec_recv.at[d],
                device_id=member_at(band, p_me, other),
                device_id_type=MESH,
            )

        for d in range(1, 4):
            spec_copy(d).start()
        spec_in[mine, :] = stage[c_me]
        for d in range(1, 4):
            spec_copy(d).wait()

        spectrum = spec_in[...]
        by_cos, by_sin = dot(cos_t[...], spectrum), dot(sin_t[...], spectrum)
        far_re = (by_cos[:, :128] + by_sin[:, 128:]) * SCALE
        far_im = (by_cos[:, 128:] - by_sin[:, :128]) * SCALE
        excess = far_re * far_re + far_im * far_im - int_t[...]
        err = jnp.concatenate(
            [(excess * far_re).astype(BF16), (excess * far_im).astype(BF16)], axis=1
        )
        by_cos, by_sin = dot(cos_t[...], err), dot(sin_t[...], err)
        back_re = ((by_cos[:, :128] - by_sin[:, 128:]) * SCALE).astype(BF16)
        back_im = ((by_cos[:, 128:] + by_sin[:, :128]) * SCALE).astype(BF16)
        for k in range(4):
            back_out[k, :, :128] = back_re[k * 128 : (k + 1) * 128]
            back_out[k, :, 128:] = back_im[k * 128 : (k + 1) * 128]

        def back_copy(d):
            other = (c_me + d) % 4
            return pltpu.make_async_remote_copy(
                src_ref=back_out.at[other],
                dst_ref=back_in.at[c_me],
                send_sem=back_send.at[d],
                recv_sem=back_recv.at[d],
                device_id=member_at(band, p_me, other),
                device_id_type=MESH,
            )

        for d in range(1, 4):
            back_copy(d).start()
        back_in[c_me] = back_out[c_me]
        for d in range(1, 4):
            back_copy(d).wait()

        back_all = jnp.concatenate(
            [
                jnp.concatenate([back_in[k, :, :128] for k in range(4)], axis=1),
                jnp.concatenate([back_in[k, :, 128:] for k in range(4)], axis=1),
            ],
            axis=0,
        )
        by_cos, by_sin = dot(back_all, cos_t[...]), dot(back_all, sin_t[...])
        gwave[0] = ((by_cos[:128] - by_sin[128:]) * SCALE).astype(BF16)
        gwave[1] = ((by_cos[128:] + by_sin[:128]) * SCALE).astype(BF16)

        def inc_target(s, j):
            return strip_at(band, s, 2 * c_me + j)

        def inc_copy(s, j):
            return pltpu.make_async_remote_copy(
                src_ref=incs.at[s, :, pl.ds(j * STRIP, STRIP), :],
                dst_ref=out.at[p_me],
                send_sem=inc_send.at[s, j],
                recv_sem=inc_recv.at[p_me],
                device_id=inc_target(s, j),
                device_id_type=MESH,
            )

        def inc_start(s):
            for j in range(2):
                local = same(inc_target(s, j), me)

                @pl.when(local)
                def _():
                    pltpu.make_async_copy(
                        incs.at[s, :, pl.ds(j * STRIP, STRIP), :], out.at[p_me], inc_recv.at[p_me]
                    ).start()

                @pl.when(jnp.logical_not(local))
                def _():
                    inc_copy(s, j).start()

        def increment(s, glit, get, put):
            seen_re, seen_im = kept(s, get)
            glit_re, glit_im = glit[:64], glit[64:]
            put(
                incs.at[s],
                glit_re * seen_re + glit_im * seen_im,
                glit_im * seen_re - glit_re * seen_im,
            )

        def pull(s, glit, get, put):
            both = get(trans.at[s]).astype(F32)
            trans_re, trans_im = both[:64], both[64:]
            glit_re, glit_im = glit[:64], glit[64:]
            put(
                gwave,
                trans_re * glit_re + trans_im * glit_im,
                trans_re * glit_im - trans_im * glit_re,
            )

        def send_rim(s):
            put_rim(gmids.at[s], *along_columns(get_rim(gwave), 1))
            halo_start(SLICES + s, gmids.at[s])

        send_rim(SLICES - 1)

        def backward(i, _):
            s = SLICES - 1 - i

            @pl.when(i > 0)
            def _():
                inc_start(s + 1)

            put_core(gmids.at[s], *along_columns(get_core(gwave), 1))
            glit = core_rows(gmids.at[s], 1)
            increment(s, glit, get_core, put_core)
            pull(s, glit, get_core, put_core)
            glit = rim_rows(SLICES + s, gmids.at[s], 1)
            pull(s, glit, get_rim, put_rim)

            @pl.when(s > 0)
            def _():
                send_rim(s - 1)

            increment(s, glit, get_rim, put_rim)
            return 0

        lax.fori_loop(0, SLICES, backward, 0)
        inc_start(0)

        def settle(s, _):
            halo_wait(s, lits.at[s], True)
            halo_wait(SLICES + s, gmids.at[s], True)
            for j in range(2):

                @pl.when(jnp.logical_not(same(inc_target(s, j), me)))
                def _():
                    inc_copy(s, j).wait_send()

            return 0

        lax.fori_loop(0, SLICES, settle, 0)

    for p in range(4):

        @pl.when(jnp.logical_not(same(member_at(band, jnp.int32(p), w // 2), me)))
        def _():
            pltpu.make_async_copy(win.at[p], win.at[p], win_send.at[p]).wait()

        @pl.when(jnp.logical_not(same(member_at(slab, jnp.int32(p), tile // 16), me)))
        def _():
            pltpu.make_async_copy(ints.at[p], ints.at[p], int_send.at[p]).wait()

        pltpu.make_async_copy(out.at[p], out.at[p], inc_recv.at[p]).wait()
    full_copy.wait()


def chain(info, phase, absorb, intensity, probe, taps):
    hbm = pl.BlockSpec(memory_space=pl.ANY)
    vmem = pl.BlockSpec(memory_space=pltpu.VMEM)
    cos_table, sin_table = (jnp.asarray(t, BF16) for t in fourier_tables())
    dma = pltpu.SemaphoreType.DMA
    group = (2, ROWS, WIN)
    return pl.pallas_call(
        chain_kernel,
        in_specs=[pl.BlockSpec(memory_space=pltpu.SMEM), hbm, hbm, hbm, hbm, vmem, hbm, hbm],
        out_specs=[hbm, hbm],
        out_shape=[
            jax.ShapeDtypeStruct((4, 2, STRIP, WIN), BF16),
            jax.ShapeDtypeStruct((2, STRIP, NXO), F32),
        ],
        scratch_shapes=[
            pltpu.VMEM((STRIP, NXO), F32),
            pltpu.VMEM((STRIP, NXO), F32),
            pltpu.VMEM((2, 8, 2, WIN), F32),
            pltpu.VMEM((2, STRIP, NXO + 512), F32),
            pltpu.VMEM((4, 2, STRIP, WIN), BF16),
            pltpu.VMEM((4, 16, WIN // 2), BF16),
            pltpu.VMEM((16, 256), F32),
            pltpu.VMEM((SLICES,) + group, BF16),
            pltpu.VMEM((SLICES + 1,) + group, BF16),
            pltpu.VMEM((SLICES,) + group, BF16),
            pltpu.VMEM((SLICES,) + group, BF16),
            pltpu.VMEM((SLICES,) + group, BF16),
            pltpu.VMEM((2 * SLICES, 2, 2, HALF, WIN), BF16),
            pltpu.VMEM((ROWS, WIN), F32),
            pltpu.VMEM(group, BF16),
            pltpu.VMEM((2, 128, 256), BF16),
            pltpu.VMEM((2, 128, 256), BF16),
            pltpu.VMEM((2, 128, 128), BF16),
            pltpu.VMEM((2, 384, 256), BF16),
            pltpu.VMEM((WIN, WIN), BF16),
            pltpu.VMEM((WIN, WIN), BF16),
            pltpu.VMEM((16, 16, WIN // 2), BF16),
            pltpu.VMEM((WIN, 128), F32),
            pltpu.VMEM((4, 128, 256), BF16),
            pltpu.VMEM((WIN, 256), BF16),
            pltpu.VMEM((4, 128, 256), BF16),
            pltpu.VMEM((4, 128, 256), BF16),
            pltpu.SemaphoreType.REGULAR,
            dma((4,)),
            dma((SLICES, 2)),
            dma((4,)),
            dma((16,)),
            dma((2 * SLICES, 2)),
            dma((2 * SLICES, 2)),
            dma((SLICES, 2)),
            dma((4,)),
            dma((4,)),
            dma((4,)),
            dma((4,)),
            dma((4,)),
            dma((3,)),
            dma((4,)),
        ],
        compiler_params=pltpu.CompilerParams(
            collective_id=0, has_side_effects=True, vmem_limit_bytes=60 << 20
        ),
        name="chain",
    )(info, phase, absorb, intensity, probe, taps, cos_table, sin_table)


def on_device(phase, absorption, probe, taps, offsets, intensity):
    band = ((lax.axis_index("tile") + 60) % 64) // 8
    info = lax.dynamic_slice_in_dim(offsets, band * 2, 2, 1).reshape(4)
    inc, trans = chain(info, phase[0], absorption[0], intensity, probe, taps)
    return finish(info, inc, trans)[None]


def solution(mesh):
    placed = (
        P("slab", "tile", None),
        P("slab", "tile", None),
        P(),
        P(),
        P(),
        P(None, "tile", None, None, None),
    )
    return jax.shard_map(
        on_device,
        mesh=mesh,
        in_specs=placed,
        out_specs=P("slab", None, "tile", None),
        check_vma=False,
    )
```
